32 devices in a mesh: groups: 2 (over x), ctx: 16 (over z, y, core).
Axes of the slice: x: 2, y: 2, z: 4, core: 2. Of those that a mesh axis runs over, the one named last changes fastest.
Arguments:
- gate_short: bfloat16 [4096, 4096], P(('groups', 'ctx')), parts along dimension 0, may hold values from -6 to 6
- key_short: bfloat16 [4096, 4096], P(('groups', 'ctx')), parts along dimension 0, may hold values from -6 to 6
- value_short: bfloat16 [4096, 4096], P(('groups', 'ctx')), parts along dimension 0, may hold values from -6 to 6
- gate_long: bfloat16 [4096, 4096], P(('groups', 'ctx')), parts along dimension 0, may hold values from -6 to 6
- doc_ids: int32 [4096], P(('groups', 'ctx')), parts along dimension 0, may hold values from 0 to 7, never falling along the last dimension, each value on 1 to 512 neighbouring positions
- se_filter: float32 [7, 256], replicated, may hold values from -2 to 2
- long_filter: bfloat16 [256, 512], replicated, may hold values from -1.25 to 1.25
Outputs:
- scored: bfloat16 [4096, 4096], P(('groups', 'ctx')), parts along dimension 0
The draws below stay inside these ranges and needn't reach their ends.
There are 2 independent parts, one for each index of `groups`. The reference program is written for one: setup_inputs(seed, part) draws one part's arguments, and reference() takes and returns one part's arrays. A program takes and returns all parts, laid end to end along the dimension named above; an argument that names none is the same for every part. Nothing has to cross between parts.
Inputs may be any that keep to these rules, and one draw needn't show every extreme that they name: doc_ids never falls along the rows of a group; each document holds 1 to 512 consecutive rows, and one holds exactly 512.
All inputs are finite; a program needn't handle non-finite values.
Results may differ from the reference program's by a relative error of at most 0.0057.
Values may be sent and summed in bfloat16 or wider, within the bound.
No kernel may reach another device: no remote copies, remote signals or barrier semaphores. Data moves between devices by JAX's collectives and lax.ppermute only.
A program may use at most 192 MiB of HBM per device.

```python
import math
import jax
import jax.numpy as jnp
import numpy as np
from jax import lax

C = 4096
FGROUP = 16
SHORT_TAPS = 7
STRETCH = 128
MAXDOC = 512
FILTERS = 256
TOKENS = 2048
DOCS = 8


def draw_long_filter(key, part):
    key_noise = jax.random.fold_in(key, 11)
    key_decay = jax.random.fold_in(key, 12)
    lag_axis = jnp.arange(MAXDOC, dtype=jnp.float32)[None, :]
    noise_draw = jax.random.truncated_normal(key_noise, -3.0, 3.0, (FILTERS, MAXDOC), jnp.float32)
    log_lowest = jnp.log(12.0)
    log_highest = jnp.log(8.0 * MAXDOC)
    decay_length = jnp.exp(jax.random.uniform(key_decay, (FILTERS, 1), jnp.float32, log_lowest, log_highest))
    norm_scale = jnp.sqrt(2.0 / jnp.minimum(decay_length, 1.0 * MAXDOC))
    return (noise_draw * jnp.exp(-lag_axis / decay_length) * norm_scale).astype(jnp.bfloat16)


def steps_of(stream_key, extent, pieces, least, top_value):
    gain, own = 1.0, jax.random.fold_in(stream_key, 6)
    for axis_at, shards_of in pieces:
        heights = jnp.exp(jax.random.uniform(jax.random.fold_in(own, axis_at), (shards_of,), jnp.float32, least / len(pieces), top_value / len(pieces)))
        gain = gain * jnp.repeat(heights, extent[axis_at] // shards_of).reshape([-1 if axis == axis_at else 1 for axis in range(len(extent))])
    return gain


def split_up(count, total, most, lean):
    loads = [(1 << 20) // math.isqrt(grade ** lean) + 1 for grade in range(2, count + 1)]
    surplus, counts = total - most - (count - 1), [1] * (count - 1)
    while surplus > 0:
        free = [i for i in range(count - 1) if counts[i] < most]
        mass, remaining = sum([loads[i] for i in free]), surplus
        for i in free:
            extra = min(most - counts[i], max(1, remaining * loads[i] // mass), surplus)
            counts[i] = counts[i] + extra
            surplus = surplus - extra
    return np.array([most] + counts)


def ragged_sizes(own_key, number_of, total, limit, skew):
    if number_of == 2:
        one = jax.random.randint(own_key, (), max(1, total - limit), min(limit, total - 1) + 1)
        return jnp.stack([one, total - one])
    sizes = jnp.asarray(split_up(number_of, total, limit, skew), jnp.int32)
    couples = (number_of - 1) // 2
    source_of, sink = sizes[1:1 + 2 * couples:2], sizes[2:2 + 2 * couples:2]
    slack = jnp.minimum(source_of - 1, limit - sink)
    moved = jax.random.randint(jax.random.fold_in(own_key, 1), (couples,), 0, 1 << 20) % (slack + 1)
    sizes = sizes.at[1:1 + 2 * couples:2].set(source_of - moved).at[2:2 + 2 * couples:2].set(sink + moved)
    return sizes[jax.random.permutation(jax.random.fold_in(own_key, 2), number_of)]


def gaussian(rng, extent, deviation, bound, cuts=(), kind=jnp.bfloat16):
    entries = deviation * jax.random.normal(rng, extent, jnp.float32)
    if cuts:
        entries = entries * steps_of(rng, extent, cuts, -0.22, 0.18)
    return jnp.clip(entries, -bound, bound).astype(kind)


def setup_inputs(seed: int = 0, part: int = 0) -> dict:
    seeds = jax.random.split(jax.random.key(seed), 8)
    part_splits = jax.random.split(jax.random.fold_in(seeds[7], part), 8)
    gate_short = gaussian(part_splits[0], (TOKENS, C), 1.0, 6.0, ((0, 16),))
    key_short = gaussian(part_splits[1], (TOKENS, C), 1.0, 6.0, ((0, 16),))
    value_short = gaussian(part_splits[2], (TOKENS, C), 1.0, 6.0, ((0, 16),))
    gate_long = gaussian(part_splits[3], (TOKENS, C), 1.0, 6.0, ((0, 16),))
    doc_ids = jnp.searchsorted(jnp.cumsum(ragged_sizes(part_splits[4], DOCS, TOKENS, MAXDOC, 2)), jnp.arange(TOKENS), side="right").astype(jnp.int32)
    se_filter = gaussian(seeds[5], (SHORT_TAPS, FILTERS), SHORT_TAPS ** -0.5, 2.0, (), jnp.float32)
    long_filter = draw_long_filter(jax.random.fold_in(seeds[7], 71), part)
    return dict(gate_short=gate_short, key_short=key_short, value_short=value_short, gate_long=gate_long, doc_ids=doc_ids, se_filter=se_filter, long_filter=long_filter)


def short_mixing(key_value, doc_ids, se_filter):
    row_count = key_value.shape[0]
    widened = jnp.repeat(se_filter, FGROUP, axis=1)
    values = key_value.astype(jnp.float32)
    summed = jnp.zeros(values.shape, jnp.float32)
    for tap_index in range(SHORT_TAPS):
        shifted = jnp.concatenate([jnp.zeros((tap_index, values.shape[1]), jnp.float32), values], 0)[:row_count]
        shifted_doc = jnp.concatenate([jnp.full((tap_index,), -1, jnp.int32), doc_ids], 0)[:row_count]
        agreeing = (shifted_doc == doc_ids).astype(jnp.float32)
        summed = summed + widened[tap_index][None, :] * agreeing[:, None] * shifted
    return summed


def long_mixing(mixed, doc_ids, long_filter):
    row_count, chan_count = mixed.shape
    filter_count = long_filter.shape[0]
    window = (MAXDOC // STRETCH + 1) * STRETCH
    front_rows = window - STRETCH
    padded = jnp.concatenate([jnp.zeros((front_rows, chan_count), mixed.dtype), mixed], 0)
    padded_doc = jnp.concatenate([jnp.full((front_rows,), -1, jnp.int32), doc_ids], 0)
    target_pos = lax.broadcasted_iota(jnp.int32, (STRETCH, window), 0)
    source_pos = lax.broadcasted_iota(jnp.int32, (STRETCH, window), 1)
    lag_table = target_pos + front_rows - source_pos
    inside = (lag_table >= 0) & (lag_table < MAXDOC)
    filter_taps = jnp.take(long_filter.astype(jnp.float32), jnp.clip(lag_table, 0, MAXDOC - 1), axis=1)
    filter_taps = jnp.where(inside[None], filter_taps, jnp.zeros_like(filter_taps))

    def one_tile(tile_index):
        begin_row = (tile_index * STRETCH).astype(jnp.int32)
        rows_win = lax.dynamic_slice_in_dim(padded, begin_row, window, 0).astype(jnp.float32)
        docs_win = lax.dynamic_slice_in_dim(padded_doc, begin_row, window, 0)
        docs_tgt = lax.dynamic_slice_in_dim(doc_ids, begin_row, STRETCH, 0)
        agreeing = (docs_tgt[:, None] == docs_win[None, :]).astype(jnp.float32)
        weights = filter_taps * agreeing[None]
        result = jnp.einsum("gtp,pgk->tgk", weights, rows_win.reshape(window, filter_count, -1))
        return result.reshape(STRETCH, chan_count)

    tile_results = lax.map(one_tile, jnp.arange(row_count // STRETCH, dtype=jnp.int32))
    return tile_results.reshape(row_count, chan_count)


def reference(gate_short, key_short, value_short, gate_long, doc_ids, se_filter, long_filter):
    key_value = (key_short.astype(jnp.float32) * value_short.astype(jnp.float32)).astype(jnp.bfloat16)
    key_value = lax.optimization_barrier(key_value)
    short_mix = short_mixing(key_value, doc_ids, se_filter)
    mixed = (gate_short.astype(jnp.float32) * short_mix).astype(jnp.bfloat16)
    mixed = lax.optimization_barrier(mixed)
    long_mix = long_mixing(mixed, doc_ids, long_filter)
    return (gate_long.astype(jnp.float32) * long_mix).astype(jnp.bfloat16)
```

```python
import functools

import jax
import jax.numpy as jnp
from jax import lax
from jax.experimental import pallas as pl
from jax.experimental.pallas import tpu as pltpu
from jax.sharding import PartitionSpec as P

F32 = jnp.float32
BF16 = jnp.bfloat16
SLAB = 16
LANES = 128
LIMIT = 40 * 1024 * 1024


def params():
    return pltpu.CompilerParams(vmem_limit_bytes=LIMIT)


def column(row):
    width = row.shape[1]
    return jnp.transpose(jnp.broadcast_to(row.astype(F32), (width, width)))


def pick(lane_group, parts):
    out = parts[0]
    for index in range(1, len(parts)):
        out = jnp.where(lane_group == index, parts[index], out)
    return out


def pack_kernel(core, key, value, gate, out):
    out[0] = (key[...].astype(F32) * value[...].astype(F32)).astype(BF16)
    out[1] = gate[...]


def short_kernel(core, docs_own, docs_sib, key, value, gate, sib, taps, mixed, mixed_a, mixed_b, tail, head,
                 kv_rows, gate_rows, agree, doc_rows):
    step = pl.program_id(0)
    rows, width = key.shape
    tap_count = taps.shape[0]
    mine = pl.multiple_of(core[0] * rows, rows)
    other = pl.multiple_of((1 - core[0]) * rows, rows)

    @pl.when(step == 0)
    def _():
        doc_rows[0:8, :] = jnp.full((8, LANES), -1.0, F32)
        doc_rows[pl.ds(8 + mine, rows), :] = column(docs_own[...])
        doc_rows[pl.ds(8 + other, rows), :] = column(docs_sib[...])
        here = doc_rows[8 : 8 + 2 * rows, :]
        for k in range(1, tap_count):
            agree[k] = (doc_rows[8 - k : 8 - k + 2 * rows, :] == here).astype(F32)
        kv_rows[0:8, :] = jnp.zeros((8, width), F32)

    kv_rows[pl.ds(8 + mine, rows), :] = (key[...].astype(F32) * value[...].astype(F32)).astype(BF16).astype(F32)
    kv_rows[pl.ds(8 + other, rows), :] = sib[0].astype(F32)
    gate_rows[pl.ds(mine, rows), :] = gate[...].astype(F32)
    gate_rows[pl.ds(other, rows), :] = sib[1].astype(F32)
    for at in range(0, width, LANES):
        cols = slice(at, at + LANES)
        total = kv_rows[8 : 8 + 2 * rows, cols] * taps[0:1, cols]
        for k in range(1, tap_count):
            total = total + agree[k] * kv_rows[8 - k : 8 - k + 2 * rows, cols] * taps[k : k + 1, cols]
        mixed[:, cols] = (gate_rows[:, cols] * total).astype(BF16)

    half = pl.num_programs(0) // 2

    @pl.when(step < half)
    def _():
        mixed_a[...] = mixed[...]

    @pl.when(step >= half)
    def _():
        mixed_b[...] = mixed[...]

    first = jnp.where(core[0] == 0, docs_own[...], docs_sib[...]).astype(F32)
    second = jnp.where(core[0] == 0, docs_sib[...], docs_own[...]).astype(F32)
    tail[0:SLAB, :] = kv_rows[8 + 2 * rows - SLAB : 8 + 2 * rows, :].astype(BF16)
    tail[SLAB : 2 * SLAB, :] = jnp.zeros((SLAB, width), BF16)
    tail[SLAB : 2 * SLAB, 0:rows] = jnp.broadcast_to(first, (SLAB, rows)).astype(BF16)
    tail[SLAB : 2 * SLAB, rows : 2 * rows] = jnp.broadcast_to(second, (SLAB, rows)).astype(BF16)
    head[0:SLAB, :] = kv_rows[8 : 8 + SLAB, :].astype(BF16)
    head[SLAB : 2 * SLAB, :] = gate_rows[0:SLAB, :].astype(BF16)


def head_kernel(tail, raw, docs, taps, out, kv_rows, doc_rows):
    rows = docs.shape[1] // 2
    tap_count = taps.shape[0]
    before = column(tail[SLAB : 2 * SLAB, rows : 2 * rows].astype(F32)[0:1])
    doc_rows[0:8, :] = before[rows - 8 :]
    doc_rows[8 : 8 + SLAB, :] = column(docs[0:1, 0:rows])[0:SLAB]
    kv_rows[0:8, :] = tail[0:SLAB, :].astype(F32)[SLAB - 8 :]
    kv_rows[8 : 8 + SLAB, :] = raw[0:SLAB, :].astype(F32)
    here = doc_rows[8 : 8 + SLAB, :]
    masks = [(doc_rows[8 - k : 8 - k + SLAB, :] == here).astype(F32) for k in range(tap_count)]
    for at in range(0, raw.shape[1], LANES):
        cols = slice(at, at + LANES)
        total = kv_rows[8 : 8 + SLAB, cols] * taps[0:1, cols]
        for k in range(1, tap_count):
            total = total + masks[k] * kv_rows[8 - k : 8 - k + SLAB, cols] * taps[k : k + 1, cols]
        out[0:SLAB, cols] = (raw[SLAB : 2 * SLAB, cols].astype(F32) * total).astype(BF16)
    out[SLAB : 2 * SLAB, :] = tail[SLAB : 2 * SLAB, :]


def strip_kernel(lags, out):
    count, width = lags.shape
    for g in range(count):
        out[g] = pltpu.roll(jnp.broadcast_to(lags[g : g + 1, :], (SLAB, width)), 0, 1, stride=1, stride_axis=0)


def far_kernel(strips, mixed, docs, out, taps, keep, groups):
    rows = docs.shape[1] // 2
    last = jnp.broadcast_to(docs[0:1, 2 * rows - 1 :].astype(F32), (rows, LANES))
    middle = jnp.broadcast_to(docs[0:1, rows - 1 : rows].astype(F32), (rows, LANES))
    summed = middle == last

    @pl.when(pl.program_id(0) == 0)
    def _():
        keep[0:rows, :] = (column(docs[0:1, 0:rows]) == last).astype(BF16)
        keep[rows:, :] = (column(docs[0:1, rows:]) == last).astype(BF16)

    lane_group = lax.broadcasted_iota(jnp.int32, (rows, LANES), 1) // (LANES // groups)
    for tile in range(mixed.shape[1] // LANES):
        cols = slice(tile * LANES, tile * LANES + LANES)
        for g in range(groups):
            for s in range(rows // SLAB):
                at = g * rows + s * SLAB
                lane = rows - SLAB * s
                taps[at : at + SLAB, :] = strips[tile * groups + g, :, lane : lane + 2 * rows]
        result = jnp.dot(taps[...], mixed[:, cols] * keep[...], preferred_element_type=F32)
        total = pick(lane_group, [result[g * rows : g * rows + rows] for g in range(groups)])
        out[:, cols] = jnp.where(summed, total, mixed[rows:, cols].astype(F32)).astype(BF16)


def own_kernel(strips, mixed, head, docs, out, diag, near, tri, keep, groups):
    rows = docs.shape[1] // 2

    @pl.when(pl.program_id(0) == 0)
    def _():
        target = lax.broadcasted_iota(jnp.int32, (rows, rows), 0)
        source = lax.broadcasted_iota(jnp.int32, (rows, rows), 1)
        lead = jnp.broadcast_to(docs[0:1, rows : rows + 1].astype(F32), (rows, rows))
        for b in range(2):
            row = docs[0:1, b * rows : b * rows + rows].astype(F32)
            col = column(row)
            tri[b] = jnp.where((col == jnp.broadcast_to(row, (rows, rows))) & (source <= target), 1.0, 0.0).astype(BF16)
            keep[b] = (col == lead).astype(F32)

    lane_group = lax.broadcasted_iota(jnp.int32, (rows, LANES), 1) // (LANES // groups)
    blank = jnp.zeros((rows, LANES), BF16)
    for tile in range(mixed.shape[1] // LANES):
        cols = slice(tile * LANES, tile * LANES + LANES)
        for g in range(groups):
            for s in range(rows // SLAB):
                at = g * rows + s * SLAB
                slab = slice(s * SLAB, s * SLAB + SLAB)
                lane = 4 * rows - SLAB * s
                both = strips[tile * groups + g, :, lane : lane + 2 * rows]
                near[at : at + SLAB, :] = both[:, 0:rows]
                diag[at : at + SLAB, 0:rows] = both[:, rows:] * tri[0, slab, :]
                diag[at : at + SLAB, rows:] = both[:, rows:] * tri[1, slab, :]
        lower = jnp.concatenate([head[0:SLAB, cols], mixed[SLAB:rows, cols]], 0)
        upper = mixed[rows:, cols]
        paired = jnp.concatenate(
            [jnp.concatenate([lower, blank], 0), jnp.concatenate([blank, upper], 0)], 1
        )
        inner = jnp.dot(diag[...], paired, preferred_element_type=F32)
        cross = jnp.dot(near[...], lower * keep[0].astype(BF16), preferred_element_type=F32)
        out[0:rows, cols] = pick(lane_group, [inner[g * rows : g * rows + rows, 0:LANES] for g in range(groups)])
        out[rows:, cols] = pick(
            lane_group, [inner[g * rows : g * rows + rows, LANES:] for g in range(groups)]
        ) + keep[1] * pick(lane_group, [cross[g * rows : g * rows + rows] for g in range(groups)])


def last_kernel(core, strips, near, fresh, prior, far, docs, own, gate_own, gate_sib, out_own, out_sib,
                taps, keep, target, total, groups):
    rows = docs.shape[1] // 2

    @pl.when(pl.program_id(0) == 0)
    def _():
        first = prior[SLAB : 2 * SLAB, 0 : 2 * rows].astype(F32)[0:1]
        second = fresh[SLAB : 2 * SLAB, 0 : 2 * rows].astype(F32)[0:1]
        end = jnp.broadcast_to(second[:, 2 * rows - 1 :], (rows, LANES))
        summed = jnp.broadcast_to(second[:, rows - 1 : rows], (rows, LANES)) == end
        for b in range(2):
            lead = jnp.broadcast_to(docs[0:1, b * rows : b * rows + 1].astype(F32), (rows, LANES))
            mine = column(docs[0:1, b * rows : b * rows + rows])
            keep[b, 0:rows, :] = ((column(second[:, rows:]) == lead) & ~summed).astype(BF16)
            keep[b, rows : 2 * rows, :] = (column(first[:, 0:rows]) == lead).astype(BF16)
            keep[b, 2 * rows :, :] = (column(first[:, rows:]) == lead).astype(BF16)
            target[b] = (mine == lead).astype(F32)
            if b == 0:
                target[2] = ((mine == end) & summed).astype(F32)

    lane_group = lax.broadcasted_iota(jnp.int32, (rows, LANES), 1) // (LANES // groups)
    blank = jnp.zeros((rows, LANES), BF16)
    for tile in range(near.shape[1] // LANES):
        cols = slice(tile * LANES, tile * LANES + LANES)
        for g in range(groups):
            for s in range(rows // SLAB):
                at = g * rows + s * SLAB
                lane = rows - SLAB * s
                taps[at : at + SLAB, :] = strips[tile * groups + g, :, lane : lane + 4 * rows]
        source = jnp.concatenate([far[:, cols], fresh[0:SLAB, cols], near[SLAB:, cols]], 0)
        paired = jnp.concatenate(
            [
                jnp.concatenate([blank, source * keep[0]], 0),
                jnp.concatenate([source * keep[1], blank], 0),
            ],
            1,
        )
        result = jnp.dot(taps[...], paired, preferred_element_type=F32)
        lower = pick(lane_group, [result[g * rows : g * rows + rows, 0:LANES] for g in range(groups)])
        upper = pick(lane_group, [result[g * rows : g * rows + rows, LANES:] for g in range(groups)])
        total[0:rows, cols] = own[0:rows, cols] + target[0] * lower + target[2] * far[:, cols].astype(F32)
        total[rows:, cols] = own[rows:, cols] + target[1] * upper
    mine = pl.multiple_of(core[0] * rows, rows)
    other = pl.multiple_of((1 - core[0]) * rows, rows)
    out_own[...] = (gate_own[...].astype(F32) * total[pl.ds(mine, rows), :]).astype(BF16)
    out_sib[...] = (gate_sib[...].astype(F32) * total[pl.ds(other, rows), :]).astype(BF16)


def body(gate_short, key_short, value_short, gate_long, doc_ids, se_filter, long_filter):
    rows, chans = gate_short.shape
    tap_count, filters = se_filter.shape
    reach = long_filter.shape[1]
    count = lax.axis_size("ctx")
    half, quarter = chans // 2, chans // 4
    group_width = chans // filters
    groups = LANES // group_width
    block = quarter // 2
    steps = half // block
    core = lax.rem(lax.axis_index("ctx"), 2)
    odd_chip = lax.rem(lax.axis_index("ctx") // 2, 2)
    core_arg = core.astype(jnp.int32).reshape(1)

    swap = [(i, i ^ 1) for i in range(count)]
    ahead = [(i, i + 2) for i in range(count - 2)]
    ahead_two = [(i, i + 4) for i in range(count - 4)]
    odd_ahead = [(i, i + 4) for i in range(count - 4) if (i // 2) % 2 == 1]
    pair = [(i, i ^ 2) for i in range(count)]

    def send(value, links):
        return lax.ppermute(value, "ctx", links)

    def full(shape):
        return pl.BlockSpec(shape, lambda i, *_: (0,) * len(shape))

    packed = pl.pallas_call(
        pack_kernel,
        grid_spec=pltpu.PrefetchScalarGridSpec(
            num_scalar_prefetch=1,
            grid=(steps,),
            in_specs=[pl.BlockSpec((rows, block), lambda i, c: (0, (1 - c[0]) * steps + i))] * 3,
            out_specs=pl.BlockSpec((2, rows, block), lambda i, c: (0, 0, i)),
        ),
        out_shape=jax.ShapeDtypeStruct((2, rows, half), BF16),
        compiler_params=params(),
        name="pack",
    )(core_arg, key_short, value_short, gate_short)
    sibling = send(packed, swap)
    docs_own = doc_ids.reshape(1, rows)
    docs_sib = send(docs_own, swap)
    docs = jnp.where(core == 0, jnp.concatenate([docs_own, docs_sib], 1), jnp.concatenate([docs_sib, docs_own], 1))

    wide_taps = jnp.repeat(
        lax.dynamic_slice_in_dim(se_filter, core * (filters // 2), filters // 2, 1), group_width, axis=1
    )
    half_filter = lax.dynamic_slice_in_dim(long_filter, core * (filters // 2), filters // 2, 0)
    lags = jnp.pad(jnp.flip(half_filter, 1), ((0, 0), (rows + 1, rows - 1)))
    strip_block = filters // 4
    strips = pl.pallas_call(
        strip_kernel,
        grid=(2,),
        in_specs=[pl.BlockSpec((strip_block, reach + 2 * rows), lambda i: (i, 0))],
        out_specs=pl.BlockSpec((strip_block, SLAB, reach + 2 * rows), lambda i: (i, 0, 0)),
        out_shape=jax.ShapeDtypeStruct((filters // 2, SLAB, reach + 2 * rows), BF16),
        compiler_params=params(),
        name="strips",
    )(lags)

    mine = pl.BlockSpec((rows, block), lambda i, c: (0, c[0] * steps + i))
    mixed, mixed_a, mixed_b, tail, raw_head = pl.pallas_call(
        short_kernel,
        grid_spec=pltpu.PrefetchScalarGridSpec(
            num_scalar_prefetch=1,
            grid=(steps,),
            in_specs=[
                full((1, rows)),
                full((1, rows)),
                mine,
                mine,
                mine,
                pl.BlockSpec((2, rows, block), lambda i, c: (0, 0, i)),
                pl.BlockSpec((tap_count, block), lambda i, c: (0, i)),
            ],
            out_specs=[
                pl.BlockSpec((2 * rows, block), lambda i, c: (0, i)),
                pl.BlockSpec((2 * rows, block), lambda i, c: (0, jnp.minimum(i, steps // 2 - 1))),
                pl.BlockSpec((2 * rows, block), lambda i, c: (0, jnp.maximum(i - steps // 2, 0))),
                pl.BlockSpec((2 * SLAB, block), lambda i, c: (0, i)),
                pl.BlockSpec((2 * SLAB, block), lambda i, c: (0, i)),
            ],
            scratch_shapes=[
                pltpu.VMEM((8 + 2 * rows, block), F32),
                pltpu.VMEM((2 * rows, block), F32),
                pltpu.VMEM((tap_count, 2 * rows, LANES), F32),
                pltpu.VMEM((8 + 2 * rows, LANES), F32),
            ],
        ),
        out_shape=[
            jax.ShapeDtypeStruct((2 * rows, half), BF16),
            jax.ShapeDtypeStruct((2 * rows, quarter), BF16),
            jax.ShapeDtypeStruct((2 * rows, quarter), BF16),
            jax.ShapeDtypeStruct((2 * SLAB, half), BF16),
            jax.ShapeDtypeStruct((2 * SLAB, half), BF16),
        ],
        compiler_params=params(),
        name="short",
    )(core_arg, docs_own, docs_sib, key_short, value_short, gate_short, sibling, wide_taps)

    relayed = send(mixed_a, odd_ahead)
    near_b = send(mixed_b, ahead)
    prior = send(tail, ahead)

    strip_spec = pl.BlockSpec((block // group_width, SLAB, reach + 2 * rows), lambda i, *_: (i, 0, 0))
    far_packet = pl.pallas_call(
        functools.partial(far_kernel, groups=groups),
        grid=(steps,),
        in_specs=[strip_spec, pl.BlockSpec((2 * rows, block), lambda i: (0, i)), full((1, 2 * rows))],
        out_specs=pl.BlockSpec((rows, block), lambda i: (0, i)),
        out_shape=jax.ShapeDtypeStruct((rows, half), BF16),
        scratch_shapes=[
            pltpu.VMEM((groups * rows, 2 * rows), BF16),
            pltpu.VMEM((2 * rows, LANES), BF16),
        ],
        compiler_params=params(),
        name="far",
    )(strips, mixed, docs)
    far = send(far_packet, ahead_two)

    head = pl.pallas_call(
        head_kernel,
        out_shape=jax.ShapeDtypeStruct((2 * SLAB, half), BF16),
        scratch_shapes=[pltpu.VMEM((8 + SLAB, half), F32), pltpu.VMEM((8 + SLAB, LANES), F32)],
        compiler_params=params(),
        name="head",
    )(prior, raw_head, docs, wide_taps)
    fresh = send(head, ahead)

    near_a = send(jnp.where(odd_chip == 1, relayed, mixed_a), pair)

    own = pl.pallas_call(
        functools.partial(own_kernel, groups=groups),
        grid=(steps,),
        in_specs=[
            strip_spec,
            pl.BlockSpec((2 * rows, block), lambda i: (0, i)),
            pl.BlockSpec((2 * SLAB, block), lambda i: (0, i)),
            full((1, 2 * rows)),
        ],
        out_specs=pl.BlockSpec((2 * rows, block), lambda i: (0, i)),
        out_shape=jax.ShapeDtypeStruct((2 * rows, half), F32),
        scratch_shapes=[
            pltpu.VMEM((groups * rows, 2 * rows), BF16),
            pltpu.VMEM((groups * rows, rows), BF16),
            pltpu.VMEM((2, rows, rows), BF16),
            pltpu.VMEM((2, rows, LANES), F32),
        ],
        compiler_params=params(),
        name="own",
    )(strips, mixed, head, docs)

    gate_sib = send(lax.dynamic_slice_in_dim(gate_long, (1 - core) * half, half, 1), swap)

    def finish(part, near):
        skip = part * (steps // 2)
        return pl.pallas_call(
            functools.partial(last_kernel, groups=groups),
            grid_spec=pltpu.PrefetchScalarGridSpec(
                num_scalar_prefetch=1,
                grid=(steps // 2,),
                in_specs=[
                    pl.BlockSpec((block // group_width, SLAB, reach + 2 * rows), lambda i, c: (i + skip, 0, 0)),
                    pl.BlockSpec((2 * rows, block), lambda i, c: (0, i)),
                    pl.BlockSpec((2 * SLAB, block), lambda i, c: (0, i + skip)),
                    full((2 * SLAB, 2 * rows)),
                    pl.BlockSpec((rows, block), lambda i, c: (0, i + skip)),
                    full((1, 2 * rows)),
                    pl.BlockSpec((2 * rows, block), lambda i, c: (0, i + skip)),
                    pl.BlockSpec((rows, block), lambda i, c: (0, c[0] * steps + i + skip)),
                    pl.BlockSpec((rows, block), lambda i, c: (0, i + skip)),
                ],
                out_specs=[pl.BlockSpec((rows, block), lambda i, c: (0, i))] * 2,
                scratch_shapes=[
                    pltpu.VMEM((groups * rows, 4 * rows), BF16),
                    pltpu.VMEM((2, 3 * rows, LANES), BF16),
                    pltpu.VMEM((3, rows, LANES), F32),
                    pltpu.VMEM((2 * rows, block), F32),
                ],
            ),
            out_shape=[jax.ShapeDtypeStruct((rows, quarter), BF16)] * 2,
            compiler_params=params(),
            name="last",
        )(core_arg, strips, near, fresh, prior, far, docs, own, gate_long, gate_sib)

    own_b, sib_b = finish(1, near_b)
    got_b = send(sib_b, swap)
    own_a, sib_a = finish(0, near_a)
    got_a = send(sib_a, swap)
    return jnp.where(
        core == 0,
        jnp.concatenate([own_a, own_b, got_a, got_b], 1),
        jnp.concatenate([got_a, got_b, own_a, own_b], 1),
    )


def solution(mesh):
    placed = (
        P(("groups", "ctx"), None),
        P(("groups", "ctx"), None),
        P(("groups", "ctx"), None),
        P(("groups", "ctx"), None),
        P(("groups", "ctx")),
        P(),
        P(),
    )
    return jax.shard_map(
        body, mesh=mesh, in_specs=placed, out_specs=P(("groups", "ctx"), None), check_vma=False
    )
```

```python
import functools

import jax
import jax.numpy as jnp
from jax import lax
from jax.experimental import pallas as pl
from jax.experimental.pallas import tpu as pltpu
from jax.sharding import PartitionSpec as P

F32 = jnp.float32
BF16 = jnp.bfloat16
SLAB = 16
LANES = 128
LIMIT = 32 * 1024 * 1024
PARTS = 2


def column(row):
    width = row.shape[1]
    return jnp.transpose(jnp.broadcast_to(row.astype(F32), (width, width)))


def pick(parts):
    lane_group = lax.broadcasted_iota(jnp.int32, parts[0].shape, 1) // (LANES // len(parts))
    out = parts[0]
    for index in range(1, len(parts)):
        out = jnp.where(lane_group == index, parts[index], out)
    return out


def widen(short_filter, first, groups):
    taps = short_filter.shape[0]
    lane = lax.broadcasted_iota(jnp.int32, (8, LANES), 1) // (LANES // groups)
    padded = jnp.concatenate([short_filter[...], jnp.zeros((8 - taps, LANES), F32)], 0)
    return jnp.take_along_axis(padded, lane + first, axis=1, mode="promise_in_bounds")


def rim_sum(tail, tail_docs, docs, taps, tap_count):
    line = lax.broadcasted_iota(jnp.int32, (8, LANES), 0)
    total = jnp.zeros((8, LANES), F32)
    for k in range(1, tap_count):
        same = (pltpu.roll(tail_docs, k, 0) == docs) & (line < k)
        total = total + jnp.where(same, pltpu.roll(tail, k, 0), 0.0) * taps[k : k + 1, :]
    return total


def build(taps, strips, tile, groups, rows, width):
    for g in range(groups):
        for s in range(rows // SLAB):
            at = g * rows + s * SLAB
            begin = rows - SLAB * s
            taps[at : at + SLAB, 0:width] = strips[tile * groups + g, :, begin : begin + width]


def pack_kernel(core, key, value, gate, out):
    out[0] = (key[...].astype(F32) * value[...].astype(F32)).astype(BF16)
    out[1] = gate[...]


def copy_kernel(core, source, after, out):
    out[...] = source[...]


def strip_kernel(core, filters, after, out):
    count, reach = filters.shape
    lane = lax.broadcasted_iota(jnp.int32, (count, LANES), 1)
    turned = []
    for at in range(reach - LANES, -1, -LANES):
        piece = filters[:, at : at + LANES].astype(F32)
        turned.append(jnp.take_along_axis(piece, LANES - 1 - lane, axis=1, mode="promise_in_bounds"))
    blank = jnp.zeros((count, LANES), F32)
    lags = jnp.concatenate([blank] + turned + [blank], 1).astype(BF16)
    for g in range(count):
        row = jnp.broadcast_to(lags[g : g + 1, :], (SLAB, lags.shape[1]))
        out[g] = pltpu.roll(row, 1, 1, stride=1, stride_axis=0)


def short_kernel(core, docs_own, docs_sib, key, value, gate, sib, short_filter, packet,
                 kv_rows, gate_rows, agree, doc_rows, groups, first_group):
    step = pl.program_id(0)
    rows, width = key.shape
    tap_count = short_filter.shape[0]
    mine = pl.multiple_of(core[0] * rows, rows)
    other = pl.multiple_of((1 - core[0]) * rows, rows)

    @pl.when(step == 0)
    def _():
        doc_rows[0:8, :] = jnp.full((8, LANES), -1.0, F32)
        doc_rows[pl.ds(8 + mine, rows), :] = column(docs_own[...])
        doc_rows[pl.ds(8 + other, rows), :] = column(docs_sib[...])
        here = doc_rows[8 : 8 + 2 * rows, :]
        for k in range(1, tap_count):
            agree[k] = (doc_rows[8 - k : 8 - k + 2 * rows, :] == here).astype(F32)
        kv_rows[0:8, :] = jnp.zeros((8, width), F32)

    kv_rows[pl.ds(8 + mine, rows), :] = (key[...].astype(F32) * value[...].astype(F32)).astype(BF16).astype(F32)
    kv_rows[pl.ds(8 + other, rows), :] = sib[0].astype(F32)
    gate_rows[pl.ds(mine, rows), :] = gate[...].astype(F32)
    gate_rows[pl.ds(other, rows), :] = sib[1].astype(F32)
    for tile in range(width // LANES):
        cols = slice(tile * LANES, tile * LANES + LANES)
        taps = widen(short_filter, first_group + (step * (width // LANES) + tile) * groups, groups)
        total = kv_rows[8 : 8 + 2 * rows, cols] * taps[0:1]
        for k in range(1, tap_count):
            total = total + agree[k] * kv_rows[8 - k : 8 - k + 2 * rows, cols] * taps[k : k + 1]
        packet[0 : 2 * rows, cols] = (gate_rows[:, cols] * total).astype(BF16)
    first = jnp.where(core[0] == 0, docs_own[...], docs_sib[...]).astype(F32)
    second = jnp.where(core[0] == 0, docs_sib[...], docs_own[...]).astype(F32)
    line = lax.broadcasted_iota(jnp.int32, (8, width), 0)
    doc_line = jnp.concatenate([first, second, jnp.zeros((1, width - 2 * rows), F32)], 1)
    tail = jnp.where(line == 0, jnp.broadcast_to(doc_line, (8, width)), kv_rows[2 * rows : 2 * rows + 8, :])
    packet[2 * rows :, :] = jnp.concatenate([tail, gate_rows[0:8, :]], 0).astype(BF16)


def far_kernel(core, strips, packet, out, taps, keep, groups):
    rows = packet.shape[0] // 2 - SLAB // 2
    docs = packet[2 * rows :, 0 : 2 * rows].astype(F32)[0:1]
    last = jnp.broadcast_to(docs[:, 2 * rows - 1 :], (rows, LANES))
    summed = jnp.broadcast_to(docs[:, rows - 1 : rows], (rows, LANES)) == last

    @pl.when(pl.program_id(0) == 0)
    def _():
        keep[0:rows, :] = (column(docs[:, 0:rows]) == last).astype(BF16)
        keep[rows:, :] = (column(docs[:, rows:]) == last).astype(BF16)

    for tile in range(out.shape[1] // LANES):
        cols = slice(tile * LANES, tile * LANES + LANES)
        build(taps.at[tile], strips, tile, groups, rows, 2 * rows)
        mixed = packet[0 : 2 * rows, cols]
        result = jnp.dot(taps[tile], mixed * keep[...], preferred_element_type=F32)
        total = pick([result[g * rows : g * rows + rows] for g in range(groups)])
        out[0:rows, cols] = jnp.where(summed, total, mixed[rows:].astype(F32)).astype(BF16)
    out[rows:, :] = packet[2 * rows :, :]


def last_kernel(core, strips, packet, near, far, short_filter, gate_own, gate_sib, *refs, groups, first_group):
    out_own, out_sib, taps, diag, tri, keep, target, total, doc_ends = refs[-9:]
    rows = far.shape[0] - SLAB
    tap_count = short_filter.shape[0]
    step = pl.program_id(0)

    @pl.when(step == 0)
    def _():
        position = lax.broadcasted_iota(jnp.int32, (rows, rows), 0)
        source = lax.broadcasted_iota(jnp.int32, (rows, rows), 1)
        docs = packet[2 * rows :, 0 : 2 * rows].astype(F32)[0:1]
        near_docs = near[2 * rows :, 0 : 2 * rows].astype(F32)[0:1]
        far_docs = far[rows:, 0 : 2 * rows].astype(F32)[0:1]
        end = jnp.broadcast_to(far_docs[:, 2 * rows - 1 :], (rows, LANES))
        summed = jnp.broadcast_to(far_docs[:, rows - 1 : rows], (rows, LANES)) == end
        here = [column(docs[:, 0:rows]), column(docs[:, rows:])]
        before = [column(far_docs[:, rows:]), column(near_docs[:, 0:rows]), column(near_docs[:, rows:])]
        for b in range(2):
            row = docs[:, b * rows : b * rows + rows]
            lead = jnp.broadcast_to(row[:, 0:1], (rows, LANES))
            same = here[b] == jnp.broadcast_to(row, (rows, rows))
            tri[b] = jnp.where(same & (source <= position), 1.0, 0.0).astype(BF16)
            keep[b, 0:rows, :] = ((before[0] == lead) & ~summed).astype(BF16)
            keep[b, rows : 2 * rows, :] = (before[1] == lead).astype(BF16)
            keep[b, 2 * rows : 3 * rows, :] = (before[2] == lead).astype(BF16)
            if b == 1:
                keep[b, 3 * rows :, :] = (here[0] == lead).astype(BF16)
            target[b] = (here[b] == lead).astype(F32)
        target[2] = ((here[0] == end) & summed).astype(F32)
        doc_ends[0] = before[2][rows - 8 :]
        doc_ends[1] = here[0][0:8]
        doc_ends[2] = before[0][rows - 8 :]
        doc_ends[3] = before[1][0:8]

    blank = jnp.zeros((rows, LANES), BF16)
    own_rim = packet[2 * rows :, :].astype(F32)
    near_rim = near[2 * rows :, :].astype(F32)
    far_rim = far[rows:, :].astype(F32)
    tiles = far.shape[1] // LANES
    for tile in range(tiles):
        cols = slice(tile * LANES, tile * LANES + LANES)
        scratch = taps.at[tile % taps.shape[0]]
        masked = diag.at[tile % taps.shape[0]]
        build(scratch, strips, tile, groups, rows, 5 * rows)
        for g in range(groups):
            here = slice(g * rows, g * rows + rows)
            masked[here, 0:rows] = scratch[here, 4 * rows :] * tri[0]
            masked[here, rows:] = scratch[here, 4 * rows :] * tri[1]
        short = widen(short_filter, first_group + (step * tiles + tile) * groups, groups)
        added = own_rim[8:, cols] * rim_sum(near_rim[0:8, cols], doc_ends[0], doc_ends[1], short, tap_count)
        lower = packet[0:rows, cols].astype(F32)
        lower = jnp.concatenate([lower[0:8] + added, lower[8:]], 0).astype(BF16)
        upper = packet[rows : 2 * rows, cols]
        added = near_rim[8:, cols] * rim_sum(far_rim[0:8, cols], doc_ends[2], doc_ends[3], short, tap_count)
        behind = near[0 : 2 * rows, cols].astype(F32)
        behind = jnp.concatenate([behind[0:8] + added, behind[8:]], 0).astype(BF16)
        source = jnp.concatenate([far[0:rows, cols], behind], 0)
        paired = jnp.concatenate(
            [jnp.concatenate([lower, blank], 0), jnp.concatenate([blank, upper], 0)], 1
        )
        inner = jnp.dot(masked[...], paired, preferred_element_type=F32)
        paired = jnp.concatenate(
            [
                jnp.concatenate([blank, source * keep[0, 0 : 3 * rows]], 0),
                jnp.concatenate([source, lower], 0) * keep[1],
            ],
            1,
        )
        outer = jnp.dot(scratch[:, 0 : 4 * rows], paired, preferred_element_type=F32)
        for b in range(2):
            side = slice(b * LANES, b * LANES + LANES)
            total[b * rows : b * rows + rows, cols] = pick(
                [inner[g * rows : g * rows + rows, side] for g in range(groups)]
            ) + target[b] * pick([outer[g * rows : g * rows + rows, side] for g in range(groups)])
        total[0:rows, cols] += target[2] * far[0:rows, cols].astype(F32)
    mine = pl.multiple_of(core[0] * rows, rows)
    other = pl.multiple_of((1 - core[0]) * rows, rows)
    out_own[...] = (gate_own[...].astype(F32) * total[pl.ds(mine, rows), :]).astype(BF16)
    out_sib[...] = (gate_sib[...].astype(F32) * total[pl.ds(other, rows), :]).astype(BF16)


def join_kernel(core, got, begun, out):
    out[...] = got[...]


def body(gate_short, key_short, value_short, gate_long, doc_ids, se_filter, long_filter):
    rows, chans = gate_short.shape
    tap_count, filters = se_filter.shape
    reach = long_filter.shape[1]
    count = lax.axis_size("ctx")
    half = chans // 2
    share = half // PARTS
    group_width = chans // filters
    groups = LANES // group_width
    block = share // 2
    steps = share // block
    width = reach + 2 * rows
    core = lax.rem(lax.axis_index("ctx"), 2).astype(jnp.int32).reshape(1)

    swap = [(i, i ^ 1) for i in range(count)]
    ahead = [(i, i + 2) for i in range(count - 2)]
    ahead_two = [(i, i + 4) for i in range(count - 4)]

    def send(value, links):
        return lax.ppermute(value, "ctx", links)

    def shape(*sizes):
        return pltpu.HBM(sizes, BF16)

    def stay(value):
        return pltpu.with_memory_space_constraint(value, pltpu.HBM)

    def whole(sizes):
        return pl.BlockSpec(sizes, lambda i, c: (0,) * len(sizes))

    def mine(height, part):
        return pl.BlockSpec((height, block), lambda i, c: (0, (PARTS * c[0] + part) * steps + i))

    def local(height):
        return pl.BlockSpec((height, block), lambda i, c: (0, i))

    def strip_part(lanes, part):
        return pl.BlockSpec((block // group_width, SLAB, lanes), lambda i, c: (part * steps + i, 0, 0))

    anywhere = pl.BlockSpec(memory_space=pl.ANY)
    short_spec = pl.BlockSpec((tap_count, filters // 2), lambda i, c: (0, c[0]))

    def call(kernel, name, grid, in_specs, out_specs, out_shape, scratch=(), aliases=None):
        return functools.partial(
            pl.pallas_call(
                kernel,
                grid_spec=pltpu.PrefetchScalarGridSpec(
                    num_scalar_prefetch=1, grid=grid, in_specs=in_specs, out_specs=out_specs, scratch_shapes=scratch
                ),
                out_shape=out_shape,
                input_output_aliases=aliases or {},
                compiler_params=pltpu.CompilerParams(vmem_limit_bytes=LIMIT),
                name=name,
            ),
            core,
        )

    gate_short, key_short, value_short, gate_long = map(stay, (gate_short, key_short, value_short, gate_long))
    docs_own = doc_ids.reshape(1, rows)
    docs_sib = send(docs_own, swap)

    def begin(part):
        return send(
            call(
                pack_kernel,
                "pack",
                (steps,),
                [pl.BlockSpec((rows, block), lambda i, c: (0, (PARTS * (1 - c[0]) + part) * steps + i))] * 3,
                pl.BlockSpec((2, rows, block), lambda i, c: (0, 0, i)),
                shape(2, rows, share),
            )(key_short, value_short, gate_short),
            swap,
        )

    def short(part, sibling):
        return call(
            functools.partial(short_kernel, groups=groups, first_group=part * (share // group_width)),
            "short",
            (steps,),
            [
                whole((1, rows)),
                whole((1, rows)),
                mine(rows, part),
                mine(rows, part),
                mine(rows, part),
                pl.BlockSpec((2, rows, block), lambda i, c: (0, 0, i)),
                short_spec,
            ],
            local(2 * rows + SLAB),
            shape(2 * rows + SLAB, share),
            [
                pltpu.VMEM((8 + 2 * rows, block), F32),
                pltpu.VMEM((2 * rows, block), F32),
                pltpu.VMEM((tap_count, 2 * rows, LANES), F32),
                pltpu.VMEM((8 + 2 * rows, LANES), F32),
            ],
        )(docs_own, docs_sib, key_short, value_short, gate_short, sibling, se_filter)

    def far_packet(part, strips, packet):
        return call(
            functools.partial(far_kernel, groups=groups),
            "far",
            (steps,),
            [strip_part(3 * rows, part), local(2 * rows + SLAB)],
            local(rows + SLAB),
            shape(rows + SLAB, share),
            [
                pltpu.VMEM((block // LANES, groups * rows, 2 * rows), BF16),
                pltpu.VMEM((2 * rows, LANES), BF16),
            ],
        )(strips, stay(packet))

    def finish(part, strips, packet, near, far, gate_sib, begun):
        return call(
            functools.partial(last_kernel, groups=groups, first_group=part * (share // group_width)),
            "last",
            (steps,),
            [
                strip_part(width, part),
                local(2 * rows + SLAB),
                local(2 * rows + SLAB),
                local(rows + SLAB),
                short_spec,
                mine(rows, part),
                pl.BlockSpec((rows, block), lambda i, c: (0, part * steps + i)),
            ]
            + [anywhere] * len(begun),
            [mine(rows, part), local(rows)],
            [shape(rows, chans), shape(rows, share)],
            [
                pltpu.VMEM((2, groups * rows, 5 * rows), BF16),
                pltpu.VMEM((2, groups * rows, 2 * rows), BF16),
                pltpu.VMEM((2, rows, rows), BF16),
                pltpu.VMEM((2, 4 * rows, LANES), BF16),
                pltpu.VMEM((3, rows, LANES), F32),
                pltpu.VMEM((2 * rows, block), F32),
                pltpu.VMEM((4, 8, LANES), F32),
            ],
            aliases={8: 0} if begun else None,
        )(strips, stay(packet), near, far, se_filter, gate_long, gate_sib, *begun)

    def join(part, got, begun):
        return call(
            join_kernel,
            "join",
            (steps,),
            [local(rows), anywhere],
            pl.BlockSpec((rows, block), lambda i, c: (0, (PARTS * (1 - c[0]) + part) * steps + i)),
            shape(rows, chans),
            aliases={2: 0},
        )(got, begun)

    siblings = [begin(part) for part in range(PARTS)]
    packets, nears, fars = [], [], []
    for part in range(PARTS):
        packet = short(part, siblings[part])
        nears.append(send(packet, ahead))
        if part == 0:
            strips = call(
                strip_kernel,
                "strips",
                (2,),
                [pl.BlockSpec((filters // 4, reach), lambda i, c: (2 * c[0] + i, 0)), anywhere],
                pl.BlockSpec((filters // 4, SLAB, width), lambda i, c: (i, 0, 0)),
                jax.ShapeDtypeStruct((filters // 2, SLAB, width), BF16),
            )(stay(long_filter), stay(packet))
        beyond = far_packet(part, strips, packet)
        fars.append(send(beyond, ahead_two))
        packets.append(packet)
    gate_sib = send(
        call(
            copy_kernel,
            "gates",
            (2,),
            [pl.BlockSpec((rows, half // 2), lambda i, c: (0, 2 * (1 - c[0]) + i)), anywhere],
            pl.BlockSpec((rows, half // 2), lambda i, c: (0, i)),
            shape(rows, half),
        )(gate_long, stay(beyond)),
        swap,
    )
    begun = ()
    for part in range(PARTS):
        out, other = finish(part, strips, packets[part], nears[part], fars[part], gate_sib, begun)
        begun = (join(part, send(other, swap), out),)
    return begun[0]


def solution(mesh):
    placed = (
        P(("groups", "ctx"), None),
        P(("groups", "ctx"), None),
        P(("groups", "ctx"), None),
        P(("groups", "ctx"), None),
        P(("groups", "ctx")),
        P(),
        P(),
    )
    return jax.shard_map(
        body, mesh=mesh, in_specs=placed, out_specs=P(("groups", "ctx"), None), check_vma=False
    )
```

```python
import functools

import jax
import jax.numpy as jnp
from jax import lax
from jax.experimental import pallas as pl
from jax.experimental.pallas import tpu as pltpu
from jax.sharding import PartitionSpec as P

F32 = jnp.float32
BF16 = jnp.bfloat16
SLAB = 16
LANES = 128
LIMIT = 32 * 1024 * 1024
PARTS = 2
STEPS = 1


def column(row):
    width = row.shape[1]
    return jnp.transpose(jnp.broadcast_to(row.astype(F32), (width, width)))


def pick(parts):
    lane_group = lax.broadcasted_iota(jnp.int32, parts[0].shape, 1) // (LANES // len(parts))
    out = parts[0]
    for index in range(1, len(parts)):
        out = jnp.where(lane_group == index, parts[index], out)
    return out


def widen(short_filter, first, groups):
    taps = short_filter.shape[0]
    lane = lax.broadcasted_iota(jnp.int32, (8, LANES), 1) // (LANES // groups)
    padded = jnp.concatenate([short_filter[...], jnp.zeros((8 - taps, LANES), F32)], 0)
    return jnp.take_along_axis(padded, lane + first, axis=1, mode="promise_in_bounds")


def rim_sum(tail, tail_docs, docs, taps, tap_count):
    line = lax.broadcasted_iota(jnp.int32, (8, LANES), 0)
    total = jnp.zeros((8, LANES), F32)
    for k in range(1, tap_count):
        same = (pltpu.roll(tail_docs, k, 0) == docs) & (line < k)
        total = total + jnp.where(same, pltpu.roll(tail, k, 0), 0.0) * taps[k : k + 1, :]
    return total


def build(taps, strips, tile, groups, rows, width, nearer=0):
    for g in range(groups):
        for s in range(rows // SLAB):
            at = g * rows + s * SLAB
            begin = (1 + nearer) * rows - SLAB * s
            taps[at : at + SLAB, 0:width] = strips[tile * groups + g, :, begin : begin + width]


def pack_kernel(core, key, value, gate, docs, out):
    rows, width = key.shape
    out[0:rows, :] = (key[...].astype(F32) * value[...].astype(F32)).astype(BF16)
    out[rows : 2 * rows, :] = gate[...]
    out[2 * rows :, 0:rows] = jnp.broadcast_to(docs[...].astype(F32), (SLAB, rows)).astype(BF16)
    out[2 * rows :, rows:] = jnp.zeros((SLAB, width - rows), BF16)


def strip_kernel(core, filters, after, out):
    count, reach = filters.shape
    lane = lax.broadcasted_iota(jnp.int32, (count, LANES), 1)
    turned = []
    for at in range(reach - LANES, -1, -LANES):
        piece = filters[:, at : at + LANES].astype(F32)
        turned.append(jnp.take_along_axis(piece, LANES - 1 - lane, axis=1, mode="promise_in_bounds"))
    blank = jnp.zeros((count, LANES), F32)
    lags = jnp.concatenate([blank] + turned + [blank], 1).astype(BF16)
    for g in range(count):
        row = jnp.broadcast_to(lags[g : g + 1, :], (SLAB, lags.shape[1]))
        out[g] = pltpu.roll(row, 1, 1, stride=1, stride_axis=0)


def short_kernel(core, docs, key, value, gate, sib, short_filter, *refs, groups, first_group):
    packet, kv_rows, gate_rows, agree, doc_rows = refs[-5:]
    step = pl.program_id(0)
    rows, width = key.shape
    tap_count = short_filter.shape[0]
    docs_own = docs[...].astype(F32)
    docs_sib = sib[2 * rows :, 0:rows].astype(F32)[0:1]
    mine = pl.multiple_of(core[0] * rows, rows)
    other = pl.multiple_of((1 - core[0]) * rows, rows)

    @pl.when(step == 0)
    def _():
        doc_rows[0:8, :] = jnp.full((8, LANES), -1.0, F32)
        doc_rows[pl.ds(8 + mine, rows), :] = column(docs_own)
        doc_rows[pl.ds(8 + other, rows), :] = column(docs_sib)
        here = doc_rows[8 : 8 + 2 * rows, :]
        for k in range(1, tap_count):
            agree[k] = (doc_rows[8 - k : 8 - k + 2 * rows, :] == here).astype(F32)
        kv_rows[0:8, :] = jnp.zeros((8, width), F32)

    kv_rows[pl.ds(8 + mine, rows), :] = (key[...].astype(F32) * value[...].astype(F32)).astype(BF16).astype(F32)
    kv_rows[pl.ds(8 + other, rows), :] = sib[0:rows, :].astype(F32)
    gate_rows[pl.ds(mine, rows), :] = gate[...].astype(F32)
    gate_rows[pl.ds(other, rows), :] = sib[rows : 2 * rows, :].astype(F32)
    for tile in range(width // LANES):
        cols = slice(tile * LANES, tile * LANES + LANES)
        taps = widen(short_filter, first_group + (step * (width // LANES) + tile) * groups, groups)
        total = kv_rows[8 : 8 + 2 * rows, cols] * taps[0:1]
        for k in range(1, tap_count):
            total = total + agree[k] * kv_rows[8 - k : 8 - k + 2 * rows, cols] * taps[k : k + 1]
        packet[0 : 2 * rows, cols] = (gate_rows[:, cols] * total).astype(BF16)
    first = jnp.where(core[0] == 0, docs_own, docs_sib)
    second = jnp.where(core[0] == 0, docs_sib, docs_own)
    line = lax.broadcasted_iota(jnp.int32, (8, width), 0)
    doc_line = jnp.concatenate([first, second, jnp.zeros((1, width - 2 * rows), F32)], 1)
    tail = jnp.where(line == 0, jnp.broadcast_to(doc_line, (8, width)), kv_rows[2 * rows : 2 * rows + 8, :])
    packet[2 * rows :, :] = jnp.concatenate([tail, gate_rows[0:8, :]], 0).astype(BF16)


def far_kernel(core, strips, packet, *refs, groups):
    out, taps, keep = refs[-3:]
    rows = packet.shape[0] // 2 - SLAB // 2
    docs = packet[2 * rows :, 0 : 2 * rows].astype(F32)[0:1]
    last = jnp.broadcast_to(docs[:, 2 * rows - 1 :], (rows, LANES))
    summed = jnp.broadcast_to(docs[:, rows - 1 : rows], (rows, LANES)) == last

    @pl.when(pl.program_id(0) == 0)
    def _():
        keep[0:rows, :] = (column(docs[:, 0:rows]) == last).astype(BF16)
        keep[rows:, :] = (column(docs[:, rows:]) == last).astype(BF16)

    for tile in range(out.shape[1] // LANES):
        cols = slice(tile * LANES, tile * LANES + LANES)
        build(taps.at[tile], strips, tile, groups, rows, 2 * rows)
        mixed = packet[0 : 2 * rows, cols]
        result = jnp.dot(taps[tile], mixed * keep[...], preferred_element_type=F32)
        total = pick([result[g * rows : g * rows + rows] for g in range(groups)])
        out[0:rows, cols] = jnp.where(summed, total, mixed[rows:].astype(F32)).astype(BF16)
    out[rows:, :] = packet[2 * rows :, :]


def block_masks(docs, near_docs, far_docs):
    rows = docs.shape[1] // 2
    here = [column(docs[:, 0:rows]), column(docs[:, rows:])]
    before = [None if far_docs is None else column(far_docs[:, rows:])]
    before += [column(near_docs[:, 0:rows]), column(near_docs[:, rows:])]
    lead = [jnp.broadcast_to(docs[:, b * rows : b * rows + 1], (rows, LANES)) for b in range(2)]
    return here, before, lead


def same_and_past(docs, col):
    rows = docs.shape[1]
    position = lax.broadcasted_iota(jnp.int32, (rows, rows), 0)
    source = lax.broadcasted_iota(jnp.int32, (rows, rows), 1)
    same = col == jnp.broadcast_to(docs, (rows, rows))
    return jnp.where(same & (source <= position), 1.0, 0.0).astype(BF16)


def far_state(far_docs):
    rows = far_docs.shape[1] // 2
    end = jnp.broadcast_to(far_docs[:, 2 * rows - 1 :], (rows, LANES))
    return end, jnp.broadcast_to(far_docs[:, rows - 1 : rows], (rows, LANES)) == end


def own_products(scratch, at, masked, tri, packet, added, cols, groups, rows):
    for g in range(groups):
        here = slice(g * rows, g * rows + rows)
        masked[here, 0:rows] = scratch[here, at:] * tri[0]
        masked[here, rows:] = scratch[here, at:] * tri[1]
    lower = packet[0:rows, cols].astype(F32)
    lower = jnp.concatenate([lower[0:8] + added, lower[8:]], 0).astype(BF16)
    blank = jnp.zeros((rows, LANES), BF16)
    paired = jnp.concatenate(
        [jnp.concatenate([lower, blank], 0), jnp.concatenate([blank, packet[rows : 2 * rows, cols]], 0)], 1
    )
    return lower, jnp.dot(masked[...], paired, preferred_element_type=F32)


def picked(result, b, groups, rows):
    side = slice(b * LANES, b * LANES + LANES)
    return pick([result[g * rows : g * rows + rows, side] for g in range(groups)])


def hand_out(core, total, gate_own, out_own, out_sib):
    rows = gate_own.shape[0]
    mine = pl.multiple_of(core[0] * rows, rows)
    other = pl.multiple_of((1 - core[0]) * rows, rows)
    out_own[...] = (gate_own[...].astype(F32) * total[pl.ds(mine, rows), :]).astype(BF16)
    out_sib[...] = total[pl.ds(other, rows), :].astype(BF16)


def middle_kernel(core, strips, packet, near, short_filter, *refs, groups, first_group):
    out, taps, diag, tri, keep, target, doc_ends = refs[-7:]
    rows = out.shape[0] // 2
    tap_count = short_filter.shape[0]
    step = pl.program_id(0)

    @pl.when(step == 0)
    def _():
        docs = packet[2 * rows :, 0 : 2 * rows].astype(F32)[0:1]
        here, before, lead = block_masks(docs, near[2 * rows :, 0 : 2 * rows].astype(F32)[0:1], None)
        for b in range(2):
            tri[b] = same_and_past(docs[:, b * rows : b * rows + rows], here[b])
            keep[b, 0:rows, :] = (before[1] == lead[b]).astype(BF16)
            keep[b, rows : 2 * rows, :] = (before[2] == lead[b]).astype(BF16)
            target[b] = (here[b] == lead[b]).astype(F32)
        keep[1, 2 * rows :, :] = (here[0] == lead[1]).astype(BF16)
        doc_ends[0] = before[2][rows - 8 :]
        doc_ends[1] = here[0][0:8]

    blank = jnp.zeros((rows, LANES), BF16)
    own_rim = packet[2 * rows :, :].astype(F32)
    near_rim = near[2 * rows :, :].astype(F32)
    tiles = out.shape[1] // LANES
    for tile in range(tiles):
        cols = slice(tile * LANES, tile * LANES + LANES)
        scratch = taps.at[tile % taps.shape[0]]
        build(scratch, strips, tile, groups, rows, 4 * rows, 1)
        short = widen(short_filter, first_group + (step * tiles + tile) * groups, groups)
        added = own_rim[8:, cols] * rim_sum(near_rim[0:8, cols], doc_ends[0], doc_ends[1], short, tap_count)
        lower, inner = own_products(
            scratch, 3 * rows, diag.at[tile % taps.shape[0]], tri, packet, added, cols, groups, rows
        )
        source = near[0 : 2 * rows, cols]
        paired = jnp.concatenate(
            [
                jnp.concatenate([blank, source * keep[0, 0 : 2 * rows]], 0),
                jnp.concatenate([source, lower], 0) * keep[1],
            ],
            1,
        )
        outer = jnp.dot(scratch[:, 0 : 3 * rows], paired, preferred_element_type=F32)
        for b in range(2):
            out[b * rows : b * rows + rows, cols] = (
                picked(inner, b, groups, rows) + target[b] * picked(outer, b, groups, rows)
            )


def rest_kernel(core, strips, packet, near, far, short_filter, gate_own, sums, *refs, groups, first_group):
    out_own, out_sib, taps, keep, target, total, doc_ends = refs[-7:]
    rows = far.shape[0] - SLAB
    tap_count = short_filter.shape[0]
    step = pl.program_id(0)

    @pl.when(step == 0)
    def _():
        docs = packet[0:SLAB, 0 : 2 * rows].astype(F32)[0:1]
        far_docs = far[rows:, 0 : 2 * rows].astype(F32)[0:1]
        here, before, lead = block_masks(docs, near[0:SLAB, 0 : 2 * rows].astype(F32)[0:1], far_docs)
        end, summed = far_state(far_docs)
        for b in range(2):
            keep[b, 0:rows, :] = ((before[0] == lead[b]) & ~summed).astype(BF16)
            keep[b, rows:, :] = (before[1] == lead[b]).astype(BF16)
            target[b] = (here[b] == lead[b]).astype(F32)
        target[2] = ((here[0] == end) & summed).astype(F32)
        doc_ends[0] = before[0][rows - 8 :]
        doc_ends[1] = before[1][0:8]

    blank = jnp.zeros((rows, LANES), BF16)
    near_rim = near[...].astype(F32)
    far_rim = far[rows:, :].astype(F32)
    tiles = far.shape[1] // LANES
    for tile in range(tiles):
        cols = slice(tile * LANES, tile * LANES + LANES)
        scratch = taps.at[tile % taps.shape[0]]
        build(scratch, strips, tile, groups, rows, 3 * rows)
        short = widen(short_filter, first_group + (step * tiles + tile) * groups, groups)
        added = near_rim[8:, cols] * rim_sum(far_rim[0:8, cols], doc_ends[0], doc_ends[1], short, tap_count)
        added = jnp.concatenate([added, jnp.zeros((rows - 8, LANES), F32)], 0).astype(BF16)
        source = jnp.concatenate([far[0:rows, cols], added], 0)
        paired = jnp.concatenate(
            [
                jnp.concatenate([blank, source * keep[0]], 0),
                jnp.concatenate([source * keep[1], blank], 0),
            ],
            1,
        )
        result = jnp.dot(scratch[...], paired, preferred_element_type=F32)
        total[0:rows, cols] = (
            sums[0:rows, cols]
            + target[0] * picked(result, 0, groups, rows)
            + target[2] * far[0:rows, cols].astype(F32)
        )
        total[rows:, cols] = sums[rows:, cols] + target[1] * picked(result, 1, groups, rows)
    hand_out(core, total, gate_own, out_own, out_sib)


def join_kernel(core, *refs):
    out = refs[-1]
    step = pl.program_id(0)
    for part in range(PARTS):

        @pl.when(step // (pl.num_programs(0) // PARTS) == part)
        def _():
            out[...] = (refs[PARTS][...].astype(F32) * refs[part][...].astype(F32)).astype(BF16)


def body(gate_short, key_short, value_short, gate_long, doc_ids, se_filter, long_filter):
    rows, chans = gate_short.shape
    tap_count, filters = se_filter.shape
    reach = long_filter.shape[1]
    count = lax.axis_size("ctx")
    half = chans // 2
    share = half // PARTS
    group_width = chans // filters
    groups = LANES // group_width
    block = share // STEPS
    steps = share // block
    width = reach + 2 * rows
    core = lax.rem(lax.axis_index("ctx"), 2).astype(jnp.int32).reshape(1)

    swap = [(i, i ^ 1) for i in range(count)]
    ahead = [(i, i + 2) for i in range(count - 2)]
    ahead_two = [(i, i + 4) for i in range(count - 4)]

    def send(value, links):
        return lax.ppermute(value, "ctx", links)

    def shape(*sizes):
        return pltpu.HBM(sizes, BF16)

    def stay(value):
        return pltpu.with_memory_space_constraint(value, pltpu.HBM)

    ahead_of = pl.Buffered(1)

    def whole(sizes):
        return pl.BlockSpec(sizes, lambda i, c: (0,) * len(sizes))

    def mine(height, part):
        return pl.BlockSpec(
            (height, block), lambda i, c: (0, (PARTS * c[0] + part) * steps + i), pipeline_mode=ahead_of
        )

    def local(height):
        return pl.BlockSpec((height, block), lambda i, c: (0, i))

    def strip_part(lanes, part):
        return pl.BlockSpec((block // group_width, SLAB, lanes), lambda i, c: (part * steps + i, 0, 0))

    anywhere = pl.BlockSpec(memory_space=pl.ANY)
    short_spec = pl.BlockSpec((tap_count, filters // 2), lambda i, c: (0, c[0]))

    def call(kernel, name, grid, in_specs, out_specs, out_shape, scratch=(), aliases=None):
        return functools.partial(
            pl.pallas_call(
                kernel,
                grid_spec=pltpu.PrefetchScalarGridSpec(
                    num_scalar_prefetch=1, grid=grid, in_specs=in_specs, out_specs=out_specs, scratch_shapes=scratch
                ),
                out_shape=out_shape,
                input_output_aliases=aliases or {},
                compiler_params=pltpu.CompilerParams(vmem_limit_bytes=LIMIT),
                name=name,
            ),
            core,
        )

    gate_short, key_short, value_short, gate_long = map(stay, (gate_short, key_short, value_short, gate_long))
    docs = stay(doc_ids.reshape(1, rows))
    se_filter = stay(se_filter)

    def begin(part):
        return send(
            call(
                pack_kernel,
                "pack",
                (steps,),
                [
                    pl.BlockSpec(
                        (rows, block),
                        lambda i, c: (0, (PARTS * (1 - c[0]) + part) * steps + i),
                        pipeline_mode=ahead_of,
                    )
                ]
                * 3
                + [whole((1, rows))],
                local(2 * rows + SLAB),
                shape(2 * rows + SLAB, share),
            )(key_short, value_short, gate_short, docs),
            swap,
        )

    def short(part, sibling, after):
        return call(
            functools.partial(short_kernel, groups=groups, first_group=part * (share // group_width)),
            "short",
            (steps,),
            [
                whole((1, rows)),
                mine(rows, part),
                mine(rows, part),
                mine(rows, part),
                local(2 * rows + SLAB),
                short_spec,
            ]
            + [anywhere] * len(after),
            local(2 * rows + SLAB),
            shape(2 * rows + SLAB, share),
            [
                pltpu.VMEM((8 + 2 * rows, block), F32),
                pltpu.VMEM((2 * rows, block), F32),
                pltpu.VMEM((tap_count, 2 * rows, LANES), F32),
                pltpu.VMEM((8 + 2 * rows, LANES), F32),
            ],
        )(docs, key_short, value_short, gate_short, sibling, se_filter, *after)

    def far_packet(part, strips, packet, after):
        return call(
            functools.partial(far_kernel, groups=groups),
            "far",
            (steps,),
            [strip_part(3 * rows, part), local(2 * rows + SLAB)] + [anywhere] * len(after),
            local(rows + SLAB),
            shape(rows + SLAB, share),
            [
                pltpu.VMEM((block // LANES, groups * rows, 2 * rows), BF16),
                pltpu.VMEM((2 * rows, LANES), BF16),
            ],
        )(strips, stay(packet), *after)

    def out_spec(part):
        return pl.BlockSpec((rows, block), lambda i, c: (0, (PARTS * c[0] + part) * steps + i))

    def middle(part, strips, packet, near):
        return call(
            functools.partial(middle_kernel, groups=groups, first_group=part * (share // group_width)),
            "middle",
            (steps,),
            [strip_part(width, part), local(2 * rows + SLAB), local(2 * rows + SLAB), short_spec],
            local(2 * rows),
            jax.ShapeDtypeStruct((2 * rows, share), F32),
            [
                pltpu.VMEM((2, groups * rows, 4 * rows), BF16),
                pltpu.VMEM((2, groups * rows, 2 * rows), BF16),
                pltpu.VMEM((2, rows, rows), BF16),
                pltpu.VMEM((2, 3 * rows, LANES), BF16),
                pltpu.VMEM((2, rows, LANES), F32),
                pltpu.VMEM((2, 8, LANES), F32),
            ],
        )(strips, stay(packet), near, se_filter)

    def rest(part, strips, packet, near, far, sums, begun, after):
        rim = pl.BlockSpec((SLAB, block), lambda i, c: (2 * rows // SLAB, i))
        return call(
            functools.partial(rest_kernel, groups=groups, first_group=part * (share // group_width)),
            "rest",
            (steps,),
            [
                strip_part(4 * rows, part),
                rim,
                rim,
                local(rows + SLAB),
                short_spec,
                mine(rows, part),
                local(2 * rows),
            ]
            + [anywhere] * len(begun + after),
            [out_spec(part), local(rows)],
            [shape(rows, chans), shape(rows, share)],
            [
                pltpu.VMEM((2, groups * rows, 3 * rows), BF16),
                pltpu.VMEM((2, 2 * rows, LANES), BF16),
                pltpu.VMEM((3, rows, LANES), F32),
                pltpu.VMEM((2 * rows, block), F32),
                pltpu.VMEM((2, 8, LANES), F32),
            ],
            aliases={8: 0} if begun else None,
        )(strips, stay(packet), near, far, se_filter, gate_long, sums, *begun, *after)

    def join(got, begun):
        there = pl.BlockSpec((rows, block), lambda i, c: (0, PARTS * steps * (1 - c[0]) + i))

        def got_spec(part):
            return pl.BlockSpec((rows, block), lambda i, c: (0, jnp.clip(i - part * steps, 0, steps - 1)))

        return call(
            join_kernel,
            "join",
            (PARTS * steps,),
            [got_spec(part) for part in range(PARTS)] + [there, anywhere],
            there,
            shape(rows, chans),
            aliases={2 + PARTS: 0},
        )(*got, gate_long, begun)

    siblings = [begin(part) for part in range(PARTS)]
    packets = [short(part, siblings[part], []) for part in range(PARTS)]
    nears = [send(packet, ahead) for packet in packets]
    strips = call(
        strip_kernel,
        "strips",
        (2,),
        [pl.BlockSpec((filters // 4, reach), lambda i, c: (2 * c[0] + i, 0)), anywhere],
        pl.BlockSpec((filters // 4, SLAB, width), lambda i, c: (i, 0, 0)),
        jax.ShapeDtypeStruct((filters // 2, SLAB, width), BF16),
    )(stay(long_filter), stay(packets[-1]))
    fars = []
    for part in range(PARTS):
        beyond = far_packet(part, strips, packets[part], [])
        fars.append(send(beyond, ahead_two))
    sums = [middle(part, strips, packets[part], nears[part]) for part in range(PARTS)]
    got, begun = [], ()
    for part in range(PARTS):
        out, other = rest(part, strips, packets[part], nears[part], fars[part], sums[part], begun, tuple(sums[part + 1 :]))
        got.append(send(other, swap))
        begun = (out,)
    return join(got, out)


def solution(mesh):
    placed = (
        P(("groups", "ctx"), None),
        P(("groups", "ctx"), None),
        P(("groups", "ctx"), None),
        P(("groups", "ctx"), None),
        P(("groups", "ctx")),
        P(),
        P(),
    )
    return jax.shard_map(
        body, mesh=mesh, in_specs=placed, out_specs=P(("groups", "ctx"), None), check_vma=False
    )
```

```python
import functools

import jax
import jax.numpy as jnp
from jax import lax
from jax.experimental import pallas as pl
from jax.experimental.pallas import tpu as pltpu
from jax.sharding import PartitionSpec as P

F32 = jnp.float32
BF16 = jnp.bfloat16
SLAB = 16
LANES = 128
LIMIT = 32 * 1024 * 1024
PARTS = 2


def column(row):
    width = row.shape[1]
    return jnp.transpose(jnp.broadcast_to(row.astype(F32), (width, width)))


def pick(parts):
    lane_group = lax.broadcasted_iota(jnp.int32, parts[0].shape, 1) // (LANES // len(parts))
    out = parts[0]
    for index in range(1, len(parts)):
        out = jnp.where(lane_group == index, parts[index], out)
    return out


def widen(short_filter, first, groups):
    taps = short_filter.shape[0]
    lane = lax.broadcasted_iota(jnp.int32, (8, LANES), 1) // (LANES // groups)
    padded = jnp.concatenate([short_filter[...], jnp.zeros((8 - taps, LANES), F32)], 0)
    return jnp.take_along_axis(padded, lane + first, axis=1, mode="promise_in_bounds")


def rim_sum(tail, tail_docs, docs, taps, tap_count):
    line = lax.broadcasted_iota(jnp.int32, (8, LANES), 0)
    total = jnp.zeros((8, LANES), F32)
    for k in range(1, tap_count):
        same = (pltpu.roll(tail_docs, k, 0) == docs) & (line < k)
        total = total + jnp.where(same, pltpu.roll(tail, k, 0), 0.0) * taps[k : k + 1, :]
    return total


def build(taps, strips, first, groups, rows, width, nearer=0):
    for g in range(groups):
        for s in range(rows // SLAB):
            at = g * rows + s * SLAB
            begin = (1 + nearer) * rows - SLAB * s
            taps[at : at + SLAB, 0:width] = strips[first + g, :, begin : begin + width]


def pack_kernel(core, key, value, gate, docs, out):
    rows, width = key.shape
    out[0:rows, :] = (key[...].astype(F32) * value[...].astype(F32)).astype(BF16)
    out[rows : 2 * rows, :] = gate[...]
    out[2 * rows :, 0:rows] = jnp.broadcast_to(docs[...].astype(F32), (SLAB, rows)).astype(BF16)
    out[2 * rows :, rows:] = jnp.zeros((SLAB, width - rows), BF16)


def strip_kernel(core, filters, after, out):
    count, reach = filters.shape
    lane = lax.broadcasted_iota(jnp.int32, (count, LANES), 1)
    turned = []
    for at in range(reach - LANES, -1, -LANES):
        piece = filters[:, at : at + LANES].astype(F32)
        turned.append(jnp.take_along_axis(piece, LANES - 1 - lane, axis=1, mode="promise_in_bounds"))
    blank = jnp.zeros((count, LANES), F32)
    lags = jnp.concatenate([blank] + turned + [blank], 1).astype(BF16)
    for g in range(count):
        row = jnp.broadcast_to(lags[g : g + 1, :], (SLAB, lags.shape[1]))
        out[g] = pltpu.roll(row, 1, 1, stride=1, stride_axis=0)


def short_kernel(core, docs, key, value, gate, sib, short_filter, *refs, groups, first_group):
    out, packet, kv_rows, gate_rows, agree, doc_rows = refs[-6:]
    step = pl.program_id(0)
    rows, width = key.shape
    tap_count = short_filter.shape[0]
    docs_own = docs[...].astype(F32)
    docs_sib = sib[2 * rows :, 0:rows].astype(F32)[0:1]
    mine = pl.multiple_of(core[0] * rows, rows)
    other = pl.multiple_of((1 - core[0]) * rows, rows)

    @pl.when(step == 0)
    def _():
        doc_rows[0:8, :] = jnp.full((8, LANES), -1.0, F32)
        doc_rows[pl.ds(8 + mine, rows), :] = column(docs_own)
        doc_rows[pl.ds(8 + other, rows), :] = column(docs_sib)
        here = doc_rows[8 : 8 + 2 * rows, :]
        for k in range(1, tap_count):
            agree[k] = (doc_rows[8 - k : 8 - k + 2 * rows, :] == here).astype(F32)
        kv_rows[0:8, :] = jnp.zeros((8, width), F32)

    kv_rows[pl.ds(8 + mine, rows), :] = (key[...].astype(F32) * value[...].astype(F32)).astype(BF16).astype(F32)
    kv_rows[pl.ds(8 + other, rows), :] = sib[0:rows, :].astype(F32)
    gate_rows[pl.ds(mine, rows), :] = gate[...].astype(F32)
    gate_rows[pl.ds(other, rows), :] = sib[rows : 2 * rows, :].astype(F32)
    for tile in range(width // LANES):
        cols = slice(tile * LANES, tile * LANES + LANES)
        taps = widen(short_filter, first_group + tile * groups, groups)
        total = kv_rows[8 : 8 + 2 * rows, cols] * taps[0:1]
        for k in range(1, tap_count):
            total = total + agree[k] * kv_rows[8 - k : 8 - k + 2 * rows, cols] * taps[k : k + 1]
        packet[0 : 2 * rows, cols] = (gate_rows[:, cols] * total).astype(BF16)
    first = jnp.where(core[0] == 0, docs_own, docs_sib)
    second = jnp.where(core[0] == 0, docs_sib, docs_own)
    line = lax.broadcasted_iota(jnp.int32, (8, width), 0)
    doc_line = jnp.concatenate([first, second, jnp.zeros((1, width - 2 * rows), F32)], 1)
    tail = jnp.where(line == 0, jnp.broadcast_to(doc_line, (8, width)), kv_rows[2 * rows : 2 * rows + 8, :])
    packet[2 * rows :, :] = jnp.concatenate([tail, gate_rows[0:8, :]], 0).astype(BF16)
    out[...] = packet[...]


def far_kernel(core, strips, packet, *refs, groups, first_group):
    out, taps, keep = refs[-3:]
    rows = packet.shape[0] // 2 - SLAB // 2
    docs = packet[2 * rows :, 0 : 2 * rows].astype(F32)[0:1]
    last = jnp.broadcast_to(docs[:, 2 * rows - 1 :], (rows, LANES))
    summed = jnp.broadcast_to(docs[:, rows - 1 : rows], (rows, LANES)) == last

    @pl.when(pl.program_id(0) == 0)
    def _():
        keep[0:rows, :] = (column(docs[:, 0:rows]) == last).astype(BF16)
        keep[rows:, :] = (column(docs[:, rows:]) == last).astype(BF16)

    for tile in range(out.shape[1] // LANES):
        cols = slice(tile * LANES, tile * LANES + LANES)
        build(taps.at[tile], strips, first_group + tile * groups, groups, rows, 2 * rows)
        mixed = packet[0 : 2 * rows, cols]
        result = jnp.dot(taps[tile], mixed * keep[...], preferred_element_type=F32)
        total = pick([result[g * rows : g * rows + rows] for g in range(groups)])
        out[0:rows, cols] = jnp.where(summed, total, mixed[rows:].astype(F32)).astype(BF16)
    out[rows:, :] = packet[2 * rows :, :]


def block_masks(docs, near_docs, far_docs):
    rows = docs.shape[1] // 2
    here = [column(docs[:, 0:rows]), column(docs[:, rows:])]
    before = [None if far_docs is None else column(far_docs[:, rows:])]
    before += [column(near_docs[:, 0:rows]), column(near_docs[:, rows:])]
    lead = [jnp.broadcast_to(docs[:, b * rows : b * rows + 1], (rows, LANES)) for b in range(2)]
    return here, before, lead


def same_and_past(docs, col):
    rows = docs.shape[1]
    position = lax.broadcasted_iota(jnp.int32, (rows, rows), 0)
    source = lax.broadcasted_iota(jnp.int32, (rows, rows), 1)
    same = col == jnp.broadcast_to(docs, (rows, rows))
    return jnp.where(same & (source <= position), 1.0, 0.0).astype(BF16)


def far_state(far_docs):
    rows = far_docs.shape[1] // 2
    end = jnp.broadcast_to(far_docs[:, 2 * rows - 1 :], (rows, LANES))
    return end, jnp.broadcast_to(far_docs[:, rows - 1 : rows], (rows, LANES)) == end


def own_products(scratch, at, masked, tri, packet, added, cols, groups, rows):
    for g in range(groups):
        here = slice(g * rows, g * rows + rows)
        masked[here, 0:rows] = scratch[here, at:] * tri[0]
        masked[here, rows:] = scratch[here, at:] * tri[1]
    lower = packet[0:rows, cols].astype(F32)
    lower = jnp.concatenate([lower[0:8] + added, lower[8:]], 0).astype(BF16)
    blank = jnp.zeros((rows, LANES), BF16)
    paired = jnp.concatenate(
        [jnp.concatenate([lower, blank], 0), jnp.concatenate([blank, packet[rows : 2 * rows, cols]], 0)], 1
    )
    return lower, jnp.dot(masked[...], paired, preferred_element_type=F32)


def picked(result, b, groups, rows):
    side = slice(b * LANES, b * LANES + LANES)
    return pick([result[g * rows : g * rows + rows, side] for g in range(groups)])


def hand_out(core, total, gate_own, out_own, out_sib):
    rows = gate_own.shape[0]
    mine = pl.multiple_of(core[0] * rows, rows)
    other = pl.multiple_of((1 - core[0]) * rows, rows)
    out_own[...] = (gate_own[...].astype(F32) * total[pl.ds(mine, rows), :]).astype(BF16)
    out_sib[...] = total[pl.ds(other, rows), :].astype(BF16)


def middle_kernel(core, strips, packet, near, short_filter, *refs, groups, first_group):
    out, taps, diag, tri, keep, target, doc_ends = refs[-7:]
    rows = out.shape[0] // 2
    tap_count = short_filter.shape[0]
    step = pl.program_id(0)

    @pl.when(step == 0)
    def _():
        docs = packet[2 * rows :, 0 : 2 * rows].astype(F32)[0:1]
        here, before, lead = block_masks(docs, near[2 * rows :, 0 : 2 * rows].astype(F32)[0:1], None)
        for b in range(2):
            tri[b] = same_and_past(docs[:, b * rows : b * rows + rows], here[b])
            keep[b, 0:rows, :] = (before[1] == lead[b]).astype(BF16)
            keep[b, rows : 2 * rows, :] = (before[2] == lead[b]).astype(BF16)
            target[b] = (here[b] == lead[b]).astype(F32)
        keep[1, 2 * rows :, :] = (here[0] == lead[1]).astype(BF16)
        doc_ends[0] = before[2][rows - 8 :]
        doc_ends[1] = here[0][0:8]

    blank = jnp.zeros((rows, LANES), BF16)
    own_rim = packet[2 * rows :, :].astype(F32)
    near_rim = near[2 * rows :, :].astype(F32)
    tiles = out.shape[1] // LANES
    for tile in range(tiles):
        cols = slice(tile * LANES, tile * LANES + LANES)
        scratch = taps.at[tile % taps.shape[0]]
        build(scratch, strips, first_group + tile * groups, groups, rows, 4 * rows, 1)
        short = widen(short_filter, first_group + tile * groups, groups)
        added = own_rim[8:, cols] * rim_sum(near_rim[0:8, cols], doc_ends[0], doc_ends[1], short, tap_count)
        lower, inner = own_products(
            scratch, 3 * rows, diag.at[tile % taps.shape[0]], tri, packet, added, cols, groups, rows
        )
        source = near[0 : 2 * rows, cols]
        paired = jnp.concatenate(
            [
                jnp.concatenate([blank, source * keep[0, 0 : 2 * rows]], 0),
                jnp.concatenate([source, lower], 0) * keep[1],
            ],
            1,
        )
        outer = jnp.dot(scratch[:, 0 : 3 * rows], paired, preferred_element_type=F32)
        for b in range(2):
            out[b * rows : b * rows + rows, cols] = (
                picked(inner, b, groups, rows) + target[b] * picked(outer, b, groups, rows)
            )


def rest_kernel(core, strips, packet, near, far, short_filter, gate_own, sums, *refs, groups, first_group):
    out_own, out_sib, taps, keep, target, total, doc_ends = refs[-7:]
    rows = far.shape[0] - SLAB
    tap_count = short_filter.shape[0]
    step = pl.program_id(0)

    @pl.when(step == 0)
    def _():
        docs = packet[0:SLAB, 0 : 2 * rows].astype(F32)[0:1]
        far_docs = far[rows:, 0 : 2 * rows].astype(F32)[0:1]
        here, before, lead = block_masks(docs, near[0:SLAB, 0 : 2 * rows].astype(F32)[0:1], far_docs)
        end, summed = far_state(far_docs)
        for b in range(2):
            keep[b, 0:rows, :] = ((before[0] == lead[b]) & ~summed).astype(BF16)
            keep[b, rows:, :] = (before[1] == lead[b]).astype(BF16)
            target[b] = (here[b] == lead[b]).astype(F32)
        target[2] = ((here[0] == end) & summed).astype(F32)
        doc_ends[0] = before[0][rows - 8 :]
        doc_ends[1] = before[1][0:8]

    blank = jnp.zeros((rows, LANES), BF16)
    near_rim = near[...].astype(F32)
    far_rim = far[rows:, :].astype(F32)
    tiles = far.shape[1] // LANES
    for tile in range(tiles):
        cols = slice(tile * LANES, tile * LANES + LANES)
        scratch = taps.at[tile % taps.shape[0]]
        build(scratch, strips, first_group + tile * groups, groups, rows, 3 * rows)
        short = widen(short_filter, first_group + tile * groups, groups)
        added = near_rim[8:, cols] * rim_sum(far_rim[0:8, cols], doc_ends[0], doc_ends[1], short, tap_count)
        added = jnp.concatenate([added, jnp.zeros((rows - 8, LANES), F32)], 0).astype(BF16)
        source = jnp.concatenate([far[0:rows, cols], added], 0)
        paired = jnp.concatenate(
            [
                jnp.concatenate([blank, source * keep[0]], 0),
                jnp.concatenate([source * keep[1], blank], 0),
            ],
            1,
        )
        result = jnp.dot(scratch[...], paired, preferred_element_type=F32)
        total[0:rows, cols] = (
            sums[0:rows, cols]
            + target[0] * picked(result, 0, groups, rows)
            + target[2] * far[0:rows, cols].astype(F32)
        )
        total[rows:, cols] = sums[rows:, cols] + target[1] * picked(result, 1, groups, rows)
    hand_out(core, total, gate_own, out_own, out_sib)


def join_kernel(core, *refs):
    out = refs[-1]
    step = pl.program_id(0)
    for part in range(PARTS):

        @pl.when(step // (pl.num_programs(0) // PARTS) == part)
        def _():
            out[...] = (refs[PARTS][...].astype(F32) * refs[part][...].astype(F32)).astype(BF16)


def body(gate_short, key_short, value_short, gate_long, doc_ids, se_filter, long_filter):
    rows, chans = gate_short.shape
    tap_count, filters = se_filter.shape
    reach = long_filter.shape[1]
    count = lax.axis_size("ctx")
    half = chans // 2
    share = half // PARTS
    group_width = chans // filters
    groups = LANES // group_width
    block, steps = share, 1
    width = reach + 2 * rows
    core = lax.rem(lax.axis_index("ctx"), 2).astype(jnp.int32).reshape(1)

    swap = [(i, i ^ 1) for i in range(count)]
    ahead = [(i, i + 2) for i in range(count - 2)]
    ahead_two = [(i, i + 4) for i in range(count - 4)]

    def send(value, links):
        return lax.ppermute(value, "ctx", links)

    def shape(*sizes):
        return pltpu.HBM(sizes, BF16)

    def stay(value):
        return pltpu.with_memory_space_constraint(value, pltpu.HBM)

    ahead_of = pl.Buffered(1)

    def whole(sizes):
        return pl.BlockSpec(sizes, lambda i, c: (0,) * len(sizes))

    def mine(height, part):
        return pl.BlockSpec(
            (height, block), lambda i, c: (0, (PARTS * c[0] + part) * steps + i), pipeline_mode=ahead_of
        )

    def local(height):
        return pl.BlockSpec((height, block), lambda i, c: (0, i))

    strip_spec = whole((filters // 2, SLAB, width))
    anywhere = pl.BlockSpec(memory_space=pl.ANY)
    short_spec = pl.BlockSpec((tap_count, filters // 2), lambda i, c: (0, c[0]))

    def call(kernel, name, grid, in_specs, out_specs, out_shape, scratch=(), aliases=None):
        return functools.partial(
            pl.pallas_call(
                kernel,
                grid_spec=pltpu.PrefetchScalarGridSpec(
                    num_scalar_prefetch=1, grid=grid, in_specs=in_specs, out_specs=out_specs, scratch_shapes=scratch
                ),
                out_shape=out_shape,
                input_output_aliases=aliases or {},
                compiler_params=pltpu.CompilerParams(vmem_limit_bytes=LIMIT),
                name=name,
            ),
            core,
        )

    gate_short, key_short, value_short = map(stay, (gate_short, key_short, value_short))
    docs = stay(doc_ids.reshape(1, rows))
    se_filter = stay(se_filter)

    def begin(part):
        return send(
            call(
                pack_kernel,
                "pack",
                (steps,),
                [
                    pl.BlockSpec(
                        (rows, block),
                        lambda i, c: (0, (PARTS * (1 - c[0]) + part) * steps + i),
                        pipeline_mode=ahead_of,
                    )
                ]
                * 3
                + [whole((1, rows))],
                local(2 * rows + SLAB),
                shape(2 * rows + SLAB, share),
            )(key_short, value_short, gate_short, docs),
            swap,
        )

    def short(part, sibling, after):
        return call(
            functools.partial(short_kernel, groups=groups, first_group=part * (share // group_width)),
            "short",
            (steps,),
            [
                whole((1, rows)),
                mine(rows, part),
                mine(rows, part),
                mine(rows, part),
                local(2 * rows + SLAB),
                short_spec,
            ]
            + [anywhere] * len(after),
            [local(2 * rows + SLAB)] * 2,
            [shape(2 * rows + SLAB, share), jax.ShapeDtypeStruct((2 * rows + SLAB, share), BF16)],
            [
                pltpu.VMEM((8 + 2 * rows, block), F32),
                pltpu.VMEM((2 * rows, block), F32),
                pltpu.VMEM((tap_count, 2 * rows, LANES), F32),
                pltpu.VMEM((8 + 2 * rows, LANES), F32),
            ],
        )(docs, key_short, value_short, gate_short, sibling, se_filter, *after)

    def far_packet(part, strips, packet, after):
        return call(
            functools.partial(far_kernel, groups=groups, first_group=part * (share // group_width)),
            "far",
            (steps,),
            [strip_spec, local(2 * rows + SLAB)] + [anywhere] * len(after),
            local(rows + SLAB),
            shape(rows + SLAB, share),
            [
                pltpu.VMEM((block // LANES, groups * rows, 2 * rows), BF16),
                pltpu.VMEM((2 * rows, LANES), BF16),
            ],
        )(strips, packet, *after)

    def out_spec(part):
        return pl.BlockSpec((rows, block), lambda i, c: (0, (PARTS * c[0] + part) * steps + i))

    def middle(part, strips, packet, near):
        return call(
            functools.partial(middle_kernel, groups=groups, first_group=part * (share // group_width)),
            "middle",
            (steps,),
            [strip_spec, local(2 * rows + SLAB), local(2 * rows + SLAB), short_spec],
            local(2 * rows),
            jax.ShapeDtypeStruct((2 * rows, share), F32),
            [
                pltpu.VMEM((2, groups * rows, 4 * rows), BF16),
                pltpu.VMEM((2, groups * rows, 2 * rows), BF16),
                pltpu.VMEM((2, rows, rows), BF16),
                pltpu.VMEM((2, 3 * rows, LANES), BF16),
                pltpu.VMEM((2, rows, LANES), F32),
                pltpu.VMEM((2, 8, LANES), F32),
            ],
        )(strips, packet, near, se_filter)

    def rest(part, strips, packet, near, far, sums, begun, after):
        rim = pl.BlockSpec((SLAB, block), lambda i, c: (2 * rows // SLAB, i))
        return call(
            functools.partial(rest_kernel, groups=groups, first_group=part * (share // group_width)),
            "rest",
            (steps,),
            [
                strip_spec,
                rim,
                rim,
                local(rows + SLAB),
                short_spec,
                mine(rows, part),
                local(2 * rows),
            ]
            + [anywhere] * len(begun + after),
            [out_spec(part), local(rows)],
            [shape(rows, chans), shape(rows, share)],
            [
                pltpu.VMEM((2, groups * rows, 3 * rows), BF16),
                pltpu.VMEM((2, 2 * rows, LANES), BF16),
                pltpu.VMEM((3, rows, LANES), F32),
                pltpu.VMEM((2 * rows, block), F32),
                pltpu.VMEM((2, 8, LANES), F32),
            ],
            aliases={8: 0} if begun else None,
        )(strips, packet, near, far, se_filter, gate_long, sums, *begun, *after)

    def join(got, begun):
        there = pl.BlockSpec((rows, block), lambda i, c: (0, PARTS * steps * (1 - c[0]) + i))

        def got_spec(part):
            return pl.BlockSpec((rows, block), lambda i, c: (0, jnp.clip(i - part * steps, 0, steps - 1)))

        return call(
            join_kernel,
            "join",
            (PARTS * steps,),
            [got_spec(part) for part in range(PARTS)] + [there, anywhere],
            there,
            shape(rows, chans),
            aliases={2 + PARTS: 0},
        )(*got, gate_long, begun)

    siblings = [begin(part) for part in range(PARTS)]
    sendable, packets = zip(*[short(part, siblings[part], []) for part in range(PARTS)])
    nears = [send(packet, ahead) for packet in sendable]
    strips = call(
        strip_kernel,
        "strips",
        (1,),
        [pl.BlockSpec((filters // 2, reach), lambda i, c: (c[0], 0)), anywhere],
        strip_spec,
        jax.ShapeDtypeStruct((filters // 2, SLAB, width), BF16),
    )(long_filter, stay(sendable[-1]))
    fars = []
    for part in range(PARTS):
        beyond = far_packet(part, strips, packets[part], [])
        fars.append(send(beyond, ahead_two))
    sums = [middle(part, strips, packets[part], nears[part]) for part in range(PARTS)]
    got, begun = [], ()
    for part in range(PARTS):
        out, other = rest(part, strips, packets[part], nears[part], fars[part], sums[part], begun, tuple(sums[part + 1 :]))
        got.append(send(other, swap))
        begun = (out,)
    return join(got, out)


def solution(mesh):
    placed = (
        P(("groups", "ctx"), None),
        P(("groups", "ctx"), None),
        P(("groups", "ctx"), None),
        P(("groups", "ctx"), None),
        P(("groups", "ctx")),
        P(),
        P(),
    )
    return jax.shard_map(
        body, mesh=mesh, in_specs=placed, out_specs=P(("groups", "ctx"), None), check_vma=False
    )
```

```python
import functools

import jax
import jax.numpy as jnp
from jax import lax
from jax.experimental import pallas as pl
from jax.experimental.pallas import tpu as pltpu
from jax.sharding import PartitionSpec as P

F32 = jnp.float32
BF16 = jnp.bfloat16
SLAB = 16
LANES = 128
LIMIT = 32 * 1024 * 1024
PARTS = 2


def column(row):
    width = row.shape[1]
    return jnp.transpose(jnp.broadcast_to(row.astype(F32), (width, width)))


def pick(parts):
    lane_group = lax.broadcasted_iota(jnp.int32, parts[0].shape, 1) // (LANES // len(parts))
    out = parts[0]
    for index in range(1, len(parts)):
        out = jnp.where(lane_group == index, parts[index], out)
    return out


def widen(short_filter, first, groups):
    taps = short_filter.shape[0]
    lane = lax.broadcasted_iota(jnp.int32, (8, LANES), 1) // (LANES // groups)
    padded = jnp.concatenate([short_filter[...], jnp.zeros((8 - taps, LANES), F32)], 0)
    return jnp.take_along_axis(padded, lane + first, axis=1, mode="promise_in_bounds")


def rim_sum(tail, tail_docs, docs, taps, tap_count):
    line = lax.broadcasted_iota(jnp.int32, (8, LANES), 0)
    total = jnp.zeros((8, LANES), F32)
    for k in range(1, tap_count):
        same = (pltpu.roll(tail_docs, k, 0) == docs) & (line < k)
        total = total + jnp.where(same, pltpu.roll(tail, k, 0), 0.0) * taps[k : k + 1, :]
    return total


def rim_rows(out, gates, tail, tail_docs, docs, short_filter, first_group, groups):
    for tile in range(out.shape[1] // LANES):
        cols = slice(tile * LANES, tile * LANES + LANES)
        taps = widen(short_filter, first_group + tile * groups, groups)
        out[:, cols] = gates[:, cols] * rim_sum(tail[:, cols], tail_docs, docs, taps, short_filter.shape[0])


def build(taps, strips, first, groups, rows, width, nearer=0):
    for g in range(groups):
        for s in range(rows // SLAB):
            at = g * rows + s * SLAB
            begin = (1 + nearer) * rows - SLAB * s
            taps[at : at + SLAB, 0:width] = strips[first + g, :, begin : begin + width]


def pack_kernel(core, key, value, gate, docs, out):
    rows, width = key.shape
    out[0:rows, :] = (key[...].astype(F32) * value[...].astype(F32)).astype(BF16)
    out[rows : 2 * rows, :] = gate[...]
    out[2 * rows :, 0:rows] = jnp.broadcast_to(docs[...].astype(F32), (SLAB, rows)).astype(BF16)
    out[2 * rows :, rows:] = jnp.zeros((SLAB, width - rows), BF16)


def strip_kernel(core, filters, after, out):
    count, reach = filters.shape
    lane = lax.broadcasted_iota(jnp.int32, (count, LANES), 1)
    turned = []
    for at in range(reach - LANES, -1, -LANES):
        piece = filters[:, at : at + LANES].astype(F32)
        turned.append(jnp.take_along_axis(piece, LANES - 1 - lane, axis=1, mode="promise_in_bounds"))
    blank = jnp.zeros((count, LANES), F32)
    lags = jnp.concatenate([blank] + turned + [blank], 1).astype(BF16)
    for g in range(count):
        row = jnp.broadcast_to(lags[g : g + 1, :], (SLAB, lags.shape[1]))
        out[g] = pltpu.roll(row, 1, 1, stride=1, stride_axis=0)


def short_kernel(core, docs, key, value, gate, sib, short_filter, *refs, groups, first_group):
    out, packet, kv_rows, gate_rows, agree, doc_rows = refs[-6:]
    step = pl.program_id(0)
    rows, width = key.shape
    tap_count = short_filter.shape[0]
    docs_own = docs[...].astype(F32)
    docs_sib = sib[2 * rows :, 0:rows].astype(F32)[0:1]
    mine = pl.multiple_of(core[0] * rows, rows)
    other = pl.multiple_of((1 - core[0]) * rows, rows)

    @pl.when(step == 0)
    def _():
        doc_rows[0:8, :] = jnp.full((8, LANES), -1.0, F32)
        doc_rows[pl.ds(8 + mine, rows), :] = column(docs_own)
        doc_rows[pl.ds(8 + other, rows), :] = column(docs_sib)
        here = doc_rows[8 : 8 + 2 * rows, :]
        for k in range(1, tap_count):
            agree[k] = (doc_rows[8 - k : 8 - k + 2 * rows, :] == here).astype(F32)
        kv_rows[0:8, :] = jnp.zeros((8, width), F32)

    kv_rows[pl.ds(8 + mine, rows), :] = (key[...].astype(F32) * value[...].astype(F32)).astype(BF16).astype(F32)
    kv_rows[pl.ds(8 + other, rows), :] = sib[0:rows, :].astype(F32)
    gate_rows[pl.ds(mine, rows), :] = gate[...].astype(F32)
    gate_rows[pl.ds(other, rows), :] = sib[rows : 2 * rows, :].astype(F32)
    for tile in range(width // LANES):
        cols = slice(tile * LANES, tile * LANES + LANES)
        taps = widen(short_filter, first_group + tile * groups, groups)
        total = kv_rows[8 : 8 + 2 * rows, cols] * taps[0:1]
        for k in range(1, tap_count):
            total = total + agree[k] * kv_rows[8 - k : 8 - k + 2 * rows, cols] * taps[k : k + 1]
        packet[0 : 2 * rows, cols] = (gate_rows[:, cols] * total).astype(BF16)
    first = jnp.where(core[0] == 0, docs_own, docs_sib)
    second = jnp.where(core[0] == 0, docs_sib, docs_own)
    line = lax.broadcasted_iota(jnp.int32, (8, width), 0)
    doc_line = jnp.concatenate([first, second, jnp.zeros((1, width - 2 * rows), F32)], 1)
    tail = jnp.where(line == 0, jnp.broadcast_to(doc_line, (8, width)), kv_rows[2 * rows : 2 * rows + 8, :])
    packet[2 * rows :, :] = jnp.concatenate([tail, gate_rows[0:8, :]], 0).astype(BF16)
    out[...] = packet[...]


def far_kernel(core, strips, packet, *refs, groups, first_group):
    out, taps, keep = refs[-3:]
    rows = packet.shape[0] // 2 - SLAB // 2
    docs = packet[2 * rows :, 0 : 2 * rows].astype(F32)[0:1]
    last = jnp.broadcast_to(docs[:, 2 * rows - 1 :], (rows, LANES))
    summed = jnp.broadcast_to(docs[:, rows + 7 : rows + 8], (rows, LANES)) == last
    tail = packet[2 * rows :, :].astype(F32)[0:8]

    @pl.when(pl.program_id(0) == 0)
    def _():
        keep[0:rows, :] = (column(docs[:, 0:rows]) == last).astype(BF16)
        keep[rows:, :] = (column(docs[:, rows:]) == last).astype(BF16)

    for tile in range(out.shape[1] // LANES):
        cols = slice(tile * LANES, tile * LANES + LANES)
        build(taps.at[tile], strips, first_group + tile * groups, groups, rows, 2 * rows)
        mixed = packet[0 : 2 * rows, cols]
        kept = mixed * keep[...]
        result = jnp.dot(taps[tile], kept, preferred_element_type=F32)
        total = pick([result[g * rows : g * rows + rows] for g in range(groups)])
        out[0:rows, cols] = jnp.where(summed, total, mixed[rows:].astype(F32)).astype(BF16)
        nearest = jnp.concatenate([taps[tile, g * rows : g * rows + SLAB, 0:rows] for g in range(groups)], 0)
        result = jnp.dot(nearest, kept[rows:], preferred_element_type=F32)
        more = pick([result[g * SLAB : g * SLAB + SLAB] for g in range(groups)])[0:8]
        out[rows:, cols] = jnp.concatenate([tail[:, cols], more], 0).astype(BF16)


def block_masks(docs, near_docs, far_docs):
    rows = docs.shape[1] // 2
    here = [column(docs[:, 0:rows]), column(docs[:, rows:])]
    before = [None if far_docs is None else column(far_docs[:, rows:])]
    before += [column(near_docs[:, 0:rows]), column(near_docs[:, rows:])]
    lead = [jnp.broadcast_to(docs[:, b * rows : b * rows + 1], (rows, LANES)) for b in range(2)]
    return here, before, lead


def same_and_past(docs, col):
    rows = docs.shape[1]
    position = lax.broadcasted_iota(jnp.int32, (rows, rows), 0)
    source = lax.broadcasted_iota(jnp.int32, (rows, rows), 1)
    same = col == jnp.broadcast_to(docs, (rows, rows))
    return jnp.where(same & (source <= position), 1.0, 0.0).astype(BF16)


def far_state(far_docs):
    rows = far_docs.shape[1] // 2
    end = jnp.broadcast_to(far_docs[:, 2 * rows - 1 :], (rows, LANES))
    return end, jnp.broadcast_to(far_docs[:, rows + 7 : rows + 8], (rows, LANES)) == end


def own_products(scratch, at, masked, tri, packet, added, cols, groups, rows):
    for g in range(groups):
        here = slice(g * rows, g * rows + rows)
        masked[here, 0:rows] = scratch[here, at:] * tri[0]
        masked[here, rows:] = scratch[here, at:] * tri[1]
    lower = packet[0:rows, cols].astype(F32)
    lower = jnp.concatenate([lower[0:8] + added, lower[8:]], 0).astype(BF16)
    blank = jnp.zeros((rows, LANES), BF16)
    paired = jnp.concatenate(
        [jnp.concatenate([lower, blank], 0), jnp.concatenate([blank, packet[rows : 2 * rows, cols]], 0)], 1
    )
    return lower, jnp.dot(masked[...], paired, preferred_element_type=F32)


def picked(result, b, groups, rows):
    side = slice(b * LANES, b * LANES + LANES)
    return pick([result[g * rows : g * rows + rows, side] for g in range(groups)])


def half_filters(core, short_filter):
    width = short_filter.shape[1] // 2
    return short_filter[:, pl.ds(pl.multiple_of(core[0] * width, LANES), width)]


def hand_out(core, total, gate_own, out_own, out_sib):
    rows = gate_own.shape[0]
    mine = pl.multiple_of(core[0] * rows, rows)
    other = pl.multiple_of((1 - core[0]) * rows, rows)
    out_own[...] = (gate_own[...].astype(F32) * total[pl.ds(mine, rows), :]).astype(BF16)
    out_sib[...] = total[pl.ds(other, rows), :].astype(BF16)


def middle_kernel(core, strips, packet, near, short_filter, *refs, groups, first_group):
    out, taps, diag, tri, keep, target, doc_ends, rim = refs[-8:]
    short_filter = half_filters(core, short_filter)
    rows = out.shape[0] // 2
    step = pl.program_id(0)

    @pl.when(step == 0)
    def _():
        docs = packet[2 * rows :, 0 : 2 * rows].astype(F32)[0:1]
        here, before, lead = block_masks(docs, near[2 * rows :, 0 : 2 * rows].astype(F32)[0:1], None)
        for b in range(2):
            tri[b] = same_and_past(docs[:, b * rows : b * rows + rows], here[b])
            keep[b, 0:rows, :] = (before[1] == lead[b]).astype(BF16)
            keep[b, rows : 2 * rows, :] = (before[2] == lead[b]).astype(BF16)
            target[b] = (here[b] == lead[b]).astype(F32)
        keep[1, 2 * rows :, :] = (here[0] == lead[1]).astype(BF16)
        doc_ends[0] = before[2][rows - 8 :]
        doc_ends[1] = here[0][0:8]

    blank = jnp.zeros((rows, LANES), BF16)
    own_rim = packet[2 * rows :, :].astype(F32)
    near_rim = near[2 * rows :, :].astype(F32)
    rim_rows(rim, own_rim[8:], near_rim[0:8], doc_ends[0], doc_ends[1], short_filter, first_group, groups)
    tiles = out.shape[1] // LANES
    for tile in range(tiles):
        cols = slice(tile * LANES, tile * LANES + LANES)
        scratch = taps.at[tile % taps.shape[0]]
        build(scratch, strips, first_group + tile * groups, groups, rows, 4 * rows, 1)
        added = rim[:, cols]
        lower, inner = own_products(
            scratch, 3 * rows, diag.at[tile % taps.shape[0]], tri, packet, added, cols, groups, rows
        )
        source = near[0 : 2 * rows, cols]
        paired = jnp.concatenate(
            [
                jnp.concatenate([blank, source * keep[0, 0 : 2 * rows]], 0),
                jnp.concatenate([source, lower], 0) * keep[1],
            ],
            1,
        )
        outer = jnp.dot(scratch[:, 0 : 3 * rows], paired, preferred_element_type=F32)
        for b in range(2):
            out[b * rows : b * rows + rows, cols] = (
                picked(inner, b, groups, rows) + target[b] * picked(outer, b, groups, rows)
            )


def rest_kernel(core, strips, packet, near, far, short_filter, gate_long, sums, *refs, groups, first_group, part):
    out_own, out_sib, taps, keep, target, total, doc_ends, rim = refs[-8:]
    short_filter = half_filters(core, short_filter)
    rows = far.shape[0] - SLAB
    step = pl.program_id(0)

    @pl.when(step == 0)
    def _():
        docs = packet[2 * rows :, 0 : 2 * rows].astype(F32)[0:1]
        far_docs = far[rows:, 0 : 2 * rows].astype(F32)[0:1]
        here, before, lead = block_masks(docs, near[2 * rows :, 0 : 2 * rows].astype(F32)[0:1], far_docs)
        end, summed = far_state(far_docs)
        for b in range(2):
            keep[b, 0:rows, :] = ((before[0] == lead[b]) & ~summed).astype(BF16)
            target[b] = (here[b] == lead[b]).astype(F32)
            target[2 + b] = ((here[b] == end) & summed).astype(F32)
            doc_ends[2 + b] = (before[1] == lead[b]).astype(F32)[0:8]
        doc_ends[0] = before[0][rows - 8 :]
        doc_ends[1] = before[1][0:8]

    lanes = lax.broadcasted_iota(jnp.int32, (SLAB, LANES), 1)
    near_rim = near[2 * rows :, :].astype(F32)
    far_rim = far[rows:, :].astype(F32)
    rim_rows(rim, near_rim[8:], far_rim[0:8], doc_ends[0], doc_ends[1], short_filter, first_group, groups)
    tiles = far.shape[1] // LANES
    for tile in range(tiles):
        cols = slice(tile * LANES, tile * LANES + LANES)
        scratch = taps.at[tile % taps.shape[0]]
        for g in range(groups):
            for slab in range(rows // SLAB):
                at = g * rows + slab * SLAB
                begin = rows - SLAB * slab
                wide = strips[first_group + tile * groups + g, :, begin : begin + 3 * rows]
                scratch[at : at + SLAB, 0:rows] = jnp.where(lanes < 8, wide[:, 2 * rows :], wide[:, 0:rows])
                scratch[at : at + SLAB, rows:] = wide[:, rows : 2 * rows]
        added = rim[:, cols]
        spread = [
            jnp.concatenate([added * doc_ends[2 + b], jnp.zeros((rows - 8, LANES), F32)], 0).astype(BF16)
            for b in range(2)
        ]
        source = far[0:rows, cols]
        paired = jnp.concatenate(
            [
                jnp.concatenate([spread[0], source * keep[0]], 0),
                jnp.concatenate([source * keep[1], spread[1]], 0),
            ],
            1,
        )
        result = jnp.dot(scratch[...], paired, preferred_element_type=F32)
        total[0:rows, cols] = (
            sums[0:rows, cols] + target[0] * picked(result, 0, groups, rows) + target[2] * source.astype(F32)
        )
        total[rows:, cols] = sums[rows:, cols] + target[1] * picked(result, 1, groups, rows)
        total[rows : rows + 8, cols] += target[3, 0:8] * far_rim[8:, cols]
    share = far.shape[1]
    at = pl.multiple_of((PARTS * core[0] + part) * share, LANES)
    hand_out(core, total, gate_long[:, pl.ds(at, share)], out_own, out_sib)


def join_kernel(core, *refs):
    out = refs[-1]
    step = pl.program_id(0)
    for part in range(PARTS):

        @pl.when(step // (pl.num_programs(0) // PARTS) == part)
        def _():
            out[...] = (refs[PARTS][...].astype(F32) * refs[part][...].astype(F32)).astype(BF16)


def body(gate_short, key_short, value_short, gate_long, doc_ids, se_filter, long_filter):
    rows, chans = gate_short.shape
    tap_count, filters = se_filter.shape
    reach = long_filter.shape[1]
    count = lax.axis_size("ctx")
    half = chans // 2
    share = half // PARTS
    group_width = chans // filters
    groups = LANES // group_width
    block, steps = share, 1
    width = reach + 2 * rows
    core = lax.rem(lax.axis_index("ctx"), 2).astype(jnp.int32).reshape(1)

    swap = [(i, i ^ 1) for i in range(count)]
    ahead = [(i, i + 2) for i in range(count - 2)]
    ahead_two = [(i, i + 4) for i in range(count - 4)]

    def send(value, links):
        return lax.ppermute(value, "ctx", links)

    def shape(*sizes):
        return pltpu.HBM(sizes, BF16)

    def stay(value):
        return pltpu.with_memory_space_constraint(value, pltpu.HBM)

    ahead_of = pl.Buffered(1)

    def whole(sizes):
        return pl.BlockSpec(sizes, lambda i, c: (0,) * len(sizes))

    def mine(height, part):
        return pl.BlockSpec(
            (height, block), lambda i, c: (0, (PARTS * c[0] + part) * steps + i), pipeline_mode=ahead_of
        )

    def local(height):
        return pl.BlockSpec((height, block), lambda i, c: (0, i))

    strip_spec = whole((filters // 2, SLAB, width))
    anywhere = pl.BlockSpec(memory_space=pl.ANY)
    short_spec = pl.BlockSpec((tap_count, filters // 2), lambda i, c: (0, c[0]))

    def call(kernel, name, grid, in_specs, out_specs, out_shape, scratch=(), aliases=None):
        return functools.partial(
            pl.pallas_call(
                kernel,
                grid_spec=pltpu.PrefetchScalarGridSpec(
                    num_scalar_prefetch=1, grid=grid, in_specs=in_specs, out_specs=out_specs, scratch_shapes=scratch
                ),
                out_shape=out_shape,
                input_output_aliases=aliases or {},
                compiler_params=pltpu.CompilerParams(vmem_limit_bytes=LIMIT),
                name=name,
            ),
            core,
        )

    gate_short, key_short, value_short = map(stay, (gate_short, key_short, value_short))
    docs = stay(doc_ids.reshape(1, rows))
    se_near, se_filter = se_filter, stay(se_filter)

    def begin(part):
        return send(
            call(
                pack_kernel,
                "pack",
                (steps,),
                [
                    pl.BlockSpec(
                        (rows, block),
                        lambda i, c: (0, (PARTS * (1 - c[0]) + part) * steps + i),
                        pipeline_mode=ahead_of,
                    )
                ]
                * 3
                + [whole((1, rows))],
                local(2 * rows + SLAB),
                shape(2 * rows + SLAB, share),
            )(key_short, value_short, gate_short, docs),
            swap,
        )

    def short(part, sibling, after):
        return call(
            functools.partial(short_kernel, groups=groups, first_group=part * (share // group_width)),
            "short",
            (steps,),
            [
                whole((1, rows)),
                mine(rows, part),
                mine(rows, part),
                mine(rows, part),
                local(2 * rows + SLAB),
                short_spec,
            ]
            + [anywhere] * len(after),
            [local(2 * rows + SLAB)] * 2,
            [shape(2 * rows + SLAB, share), jax.ShapeDtypeStruct((2 * rows + SLAB, share), BF16)],
            [
                pltpu.VMEM((8 + 2 * rows, block), F32),
                pltpu.VMEM((2 * rows, block), F32),
                pltpu.VMEM((tap_count, 2 * rows, LANES), F32),
                pltpu.VMEM((8 + 2 * rows, LANES), F32),
            ],
        )(docs, key_short, value_short, gate_short, sibling, se_filter, *after)

    def far_packet(part, strips, packet, after):
        return call(
            functools.partial(far_kernel, groups=groups, first_group=part * (share // group_width)),
            "far",
            (steps,),
            [strip_spec, local(2 * rows + SLAB)] + [anywhere] * len(after),
            local(rows + SLAB),
            shape(rows + SLAB, share),
            [
                pltpu.VMEM((block // LANES, groups * rows, 2 * rows), BF16),
                pltpu.VMEM((2 * rows, LANES), BF16),
            ],
        )(strips, packet, *after)

    def out_spec(part):
        return pl.BlockSpec((rows, block), lambda i, c: (0, (PARTS * c[0] + part) * steps + i))

    def middle(part, strips, packet, near):
        return call(
            functools.partial(middle_kernel, groups=groups, first_group=part * (share // group_width)),
            "middle",
            (steps,),
            [strip_spec, local(2 * rows + SLAB), local(2 * rows + SLAB), whole((tap_count, filters))],
            local(2 * rows),
            jax.ShapeDtypeStruct((2 * rows, share), F32),
            [
                pltpu.VMEM((2, groups * rows, 4 * rows), BF16),
                pltpu.VMEM((2, groups * rows, 2 * rows), BF16),
                pltpu.VMEM((2, rows, rows), BF16),
                pltpu.VMEM((2, 3 * rows, LANES), BF16),
                pltpu.VMEM((2, rows, LANES), F32),
                pltpu.VMEM((2, 8, LANES), F32),
                pltpu.VMEM((8, share), F32),
            ],
        )(strips, packet, near, se_near)

    def rest(part, strips, packet, near, far, sums, begun, after):
        return call(
            functools.partial(rest_kernel, groups=groups, first_group=part * (share // group_width), part=part),
            "rest",
            (steps,),
            [
                strip_spec,
                local(2 * rows + SLAB),
                local(2 * rows + SLAB),
                local(rows + SLAB),
                whole((tap_count, filters)),
                whole((rows, chans)),
                local(2 * rows),
            ]
            + [anywhere] * len(begun + after),
            [out_spec(part), local(rows)],
            [shape(rows, chans), shape(rows, share)],
            [
                pltpu.VMEM((2, groups * rows, 2 * rows), BF16),
                pltpu.VMEM((2, rows, LANES), BF16),
                pltpu.VMEM((4, rows, LANES), F32),
                pltpu.VMEM((2 * rows, block), F32),
                pltpu.VMEM((4, 8, LANES), F32),
                pltpu.VMEM((8, share), F32),
            ],
            aliases={8: 0} if begun else None,
        )(strips, packet, near, far, se_near, gate_long, sums, *begun, *after)

    def join(got, begun):
        there = pl.BlockSpec((rows, block), lambda i, c: (0, PARTS * steps * (1 - c[0]) + i))

        def got_spec(part):
            return pl.BlockSpec((rows, block), lambda i, c: (0, jnp.clip(i - part * steps, 0, steps - 1)))

        return call(
            join_kernel,
            "join",
            (PARTS * steps,),
            [got_spec(part) for part in range(PARTS)] + [there, anywhere],
            there,
            shape(rows, chans),
            aliases={2 + PARTS: 0},
        )(*got, gate_long, begun)

    siblings = [begin(part) for part in range(PARTS)]
    sendable, packets = zip(*[short(part, siblings[part], []) for part in range(PARTS)])
    nears = [send(packet, ahead) for packet in sendable]
    strips = call(
        strip_kernel,
        "strips",
        (1,),
        [pl.BlockSpec((filters // 2, reach), lambda i, c: (c[0], 0)), anywhere],
        strip_spec,
        jax.ShapeDtypeStruct((filters // 2, SLAB, width), BF16),
    )(long_filter, stay(sendable[-1]))
    fars = []
    for part in range(PARTS):
        beyond = far_packet(part, strips, packets[part], [])
        fars.append(send(beyond, ahead_two))
    sums = [middle(part, strips, packets[part], nears[part]) for part in range(PARTS)]
    got, begun = [], ()
    for part in range(PARTS):
        out, other = rest(part, strips, packets[part], nears[part], fars[part], sums[part], begun, tuple(sums[part + 1 :]))
        got.append(send(other, swap))
        begun = (out,)
    return join(got, out)


def solution(mesh):
    placed = (
        P(("groups", "ctx"), None),
        P(("groups", "ctx"), None),
        P(("groups", "ctx"), None),
        P(("groups", "ctx"), None),
        P(("groups", "ctx")),
        P(),
        P(),
    )
    return jax.shard_map(
        body, mesh=mesh, in_specs=placed, out_specs=P(("groups", "ctx"), None), check_vma=False
    )
```

```python
import functools

import jax
import jax.numpy as jnp
from jax import lax
from jax.experimental import pallas as pl
from jax.experimental.pallas import tpu as pltpu
from jax.sharding import PartitionSpec as P

F32 = jnp.float32
BF16 = jnp.bfloat16
SLAB = 16
LANES = 128
LIMIT = 32 * 1024 * 1024
PARTS = 2


def column(row):
    width = row.shape[1]
    return jnp.transpose(jnp.broadcast_to(row.astype(F32), (width, width)))


def pick(parts):
    lane_group = lax.broadcasted_iota(jnp.int32, parts[0].shape, 1) // (LANES // len(parts))
    out = parts[0]
    for index in range(1, len(parts)):
        out = jnp.where(lane_group == index, parts[index], out)
    return out


def widen(short_filter, first, groups):
    taps = short_filter.shape[0]
    lane = lax.broadcasted_iota(jnp.int32, (8, LANES), 1) // (LANES // groups)
    padded = jnp.concatenate([short_filter[...], jnp.zeros((8 - taps, LANES), F32)], 0)
    return jnp.take_along_axis(padded, lane + first, axis=1, mode="promise_in_bounds")


def rim_sum(tail, tail_docs, docs, taps, tap_count):
    line = lax.broadcasted_iota(jnp.int32, (8, LANES), 0)
    total = jnp.zeros((8, LANES), F32)
    for k in range(1, tap_count):
        same = (pltpu.roll(tail_docs, k, 0) == docs) & (line < k)
        total = total + jnp.where(same, pltpu.roll(tail, k, 0), 0.0) * taps[k : k + 1, :]
    return total


def rim_rows(out, gates, tail, tail_docs, docs, short_filter, first_group, groups):
    for tile in range(out.shape[1] // LANES):
        cols = slice(tile * LANES, tile * LANES + LANES)
        taps = widen(short_filter, first_group + tile * groups, groups)
        out[:, cols] = gates[:, cols] * rim_sum(tail[:, cols], tail_docs, docs, taps, short_filter.shape[0])


def build(taps, strips, first, groups, rows, width):
    for g in range(groups):
        for s in range(rows // SLAB):
            at = g * rows + s * SLAB
            begin = rows - SLAB * s
            taps[at : at + SLAB, 0:width] = strips[first + g, :, begin : begin + width]


def pack_kernel(core, key, value, gate, docs, out):
    rows, width = key.shape
    out[0:rows, :] = (key[...].astype(F32) * value[...].astype(F32)).astype(BF16)
    out[rows : 2 * rows, :] = gate[...]
    out[2 * rows :, 0:rows] = jnp.broadcast_to(docs[...].astype(F32), (SLAB, rows)).astype(BF16)
    out[2 * rows :, rows:] = jnp.zeros((SLAB, width - rows), BF16)


def strip_kernel(core, filters, after, out):
    count, reach = filters.shape
    lane = lax.broadcasted_iota(jnp.int32, (count, LANES), 1)
    turned = []
    for at in range(reach - LANES, -1, -LANES):
        piece = filters[:, at : at + LANES].astype(F32)
        turned.append(jnp.take_along_axis(piece, LANES - 1 - lane, axis=1, mode="promise_in_bounds"))
    blank = jnp.zeros((count, LANES), F32)
    lags = jnp.concatenate([blank] + turned + [blank], 1).astype(BF16)
    for g in range(count):
        row = jnp.broadcast_to(lags[g : g + 1, :], (SLAB, lags.shape[1]))
        out[g] = pltpu.roll(row, 1, 1, stride=1, stride_axis=0)


def short_kernel(core, docs, key, value, gate, sib, short_filter, *refs, groups, first_group):
    out, packet, kv_rows, gate_rows, agree, doc_rows = refs[-6:]
    step = pl.program_id(0)
    rows, width = key.shape
    tap_count = short_filter.shape[0]
    docs_own = docs[...].astype(F32)
    docs_sib = sib[2 * rows :, 0:rows].astype(F32)[0:1]
    mine = pl.multiple_of(core[0] * rows, rows)
    other = pl.multiple_of((1 - core[0]) * rows, rows)

    @pl.when(step == 0)
    def _():
        doc_rows[0:8, :] = jnp.full((8, LANES), -1.0, F32)
        doc_rows[pl.ds(8 + mine, rows), :] = column(docs_own)
        doc_rows[pl.ds(8 + other, rows), :] = column(docs_sib)
        here = doc_rows[8 : 8 + 2 * rows, :]
        for k in range(1, tap_count):
            agree[k] = (doc_rows[8 - k : 8 - k + 2 * rows, :] == here).astype(F32)
        kv_rows[0:8, :] = jnp.zeros((8, width), F32)

    kv_rows[pl.ds(8 + mine, rows), :] = (key[...].astype(F32) * value[...].astype(F32)).astype(BF16).astype(F32)
    kv_rows[pl.ds(8 + other, rows), :] = sib[0:rows, :].astype(F32)
    gate_rows[pl.ds(mine, rows), :] = gate[...].astype(F32)
    gate_rows[pl.ds(other, rows), :] = sib[rows : 2 * rows, :].astype(F32)
    for tile in range(width // LANES):
        cols = slice(tile * LANES, tile * LANES + LANES)
        taps = widen(short_filter, first_group + tile * groups, groups)
        total = kv_rows[8 : 8 + 2 * rows, cols] * taps[0:1]
        for k in range(1, tap_count):
            total = total + agree[k] * kv_rows[8 - k : 8 - k + 2 * rows, cols] * taps[k : k + 1]
        packet[0 : 2 * rows, cols] = (gate_rows[:, cols] * total).astype(BF16)
    first = jnp.where(core[0] == 0, docs_own, docs_sib)
    second = jnp.where(core[0] == 0, docs_sib, docs_own)
    line = lax.broadcasted_iota(jnp.int32, (8, width), 0)
    doc_line = jnp.concatenate([first, second, jnp.zeros((1, width - 2 * rows), F32)], 1)
    tail = jnp.where(line == 0, jnp.broadcast_to(doc_line, (8, width)), kv_rows[2 * rows : 2 * rows + 8, :])
    packet[2 * rows :, :] = jnp.concatenate([tail, gate_rows[0:8, :]], 0).astype(BF16)
    out[...] = packet[...]


def far_kernel(core, strips, packet, *refs, groups, first_group):
    out, taps, keep = refs[-3:]
    rows = packet.shape[0] // 2 - SLAB // 2
    docs = packet[2 * rows :, 0 : 2 * rows].astype(F32)[0:1]
    last = jnp.broadcast_to(docs[:, 2 * rows - 1 :], (rows, LANES))
    summed = jnp.broadcast_to(docs[:, rows + 7 : rows + 8], (rows, LANES)) == last
    tail = packet[2 * rows :, :].astype(F32)[0:8]

    @pl.when(pl.program_id(0) == 0)
    def _():
        keep[0:rows, :] = (column(docs[:, 0:rows]) == last).astype(BF16)
        keep[rows:, :] = (column(docs[:, rows:]) == last).astype(BF16)

    for tile in range(out.shape[1] // LANES):
        cols = slice(tile * LANES, tile * LANES + LANES)
        build(taps.at[tile], strips, first_group + tile * groups, groups, rows, 2 * rows)
        mixed = packet[0 : 2 * rows, cols]
        kept = mixed * keep[...]
        result = jnp.dot(taps[tile], kept, preferred_element_type=F32)
        total = pick([result[g * rows : g * rows + rows] for g in range(groups)])
        out[0:rows, cols] = jnp.where(summed, total, mixed[rows:].astype(F32)).astype(BF16)
        nearest = jnp.concatenate([taps[tile, g * rows : g * rows + SLAB, 0:rows] for g in range(groups)], 0)
        result = jnp.dot(nearest, kept[rows:], preferred_element_type=F32)
        more = pick([result[g * SLAB : g * SLAB + SLAB] for g in range(groups)])[0:8]
        out[rows:, cols] = jnp.concatenate([tail[:, cols], more], 0).astype(BF16)


def block_masks(docs, near_docs, far_docs):
    rows = docs.shape[1] // 2
    here = [column(docs[:, 0:rows]), column(docs[:, rows:])]
    before = [None if far_docs is None else column(far_docs[:, rows:])]
    before += [column(near_docs[:, 0:rows]), column(near_docs[:, rows:])]
    lead = [jnp.broadcast_to(docs[:, b * rows : b * rows + 1], (rows, LANES)) for b in range(2)]
    return here, before, lead


def same_and_past(docs, col):
    rows = docs.shape[1]
    position = lax.broadcasted_iota(jnp.int32, (rows, rows), 0)
    source = lax.broadcasted_iota(jnp.int32, (rows, rows), 1)
    same = col == jnp.broadcast_to(docs, (rows, rows))
    return jnp.where(same & (source <= position), 1.0, 0.0).astype(BF16)


def far_state(far_docs):
    rows = far_docs.shape[1] // 2
    end = jnp.broadcast_to(far_docs[:, 2 * rows - 1 :], (rows, LANES))
    return end, jnp.broadcast_to(far_docs[:, rows + 7 : rows + 8], (rows, LANES)) == end


def build_middle(scratch, masked, tri, strips, first, groups, rows):
    for g in range(groups):
        for slab in range(rows // SLAB):
            at = g * rows + slab * SLAB
            begin = 2 * rows - SLAB * slab
            wide = strips[first + g, :, begin : begin + 4 * rows]
            scratch[at : at + SLAB, :] = wide[:, 0 : 3 * rows]
            inside = wide[:, 3 * rows :]
            for b in range(2):
                side = slice(b * rows, b * rows + rows)
                masked[at : at + SLAB, side] = inside * tri[b, slab * SLAB : slab * SLAB + SLAB, :]


def own_products(masked, packet, added, cols, rows):
    lower = packet[0:rows, cols].astype(F32)
    lower = jnp.concatenate([lower[0:8] + added, lower[8:]], 0).astype(BF16)
    blank = jnp.zeros((rows, LANES), BF16)
    paired = jnp.concatenate(
        [jnp.concatenate([lower, blank], 0), jnp.concatenate([blank, packet[rows : 2 * rows, cols]], 0)], 1
    )
    return lower, jnp.dot(masked[...], paired, preferred_element_type=F32)


def picked(result, b, groups, rows):
    side = slice(b * LANES, b * LANES + LANES)
    return pick([result[g * rows : g * rows + rows, side] for g in range(groups)])


def half_filters(core, short_filter):
    width = short_filter.shape[1] // 2
    return short_filter[:, pl.ds(pl.multiple_of(core[0] * width, LANES), width)]


def hand_out(core, total, gate_own, out_own, out_sib):
    rows = gate_own.shape[0]
    mine = pl.multiple_of(core[0] * rows, rows)
    other = pl.multiple_of((1 - core[0]) * rows, rows)
    out_own[...] = (gate_own[...].astype(F32) * total[pl.ds(mine, rows), :]).astype(BF16)
    out_sib[...] = total[pl.ds(other, rows), :].astype(BF16)


def middle_kernel(core, strips, packet, near, short_filter, *refs, groups, first_group):
    out, taps, diag, tri, keep, target, doc_ends, rim = refs[-8:]
    short_filter = half_filters(core, short_filter)
    rows = out.shape[0] // 2
    step = pl.program_id(0)

    @pl.when(step == 0)
    def _():
        docs = packet[2 * rows :, 0 : 2 * rows].astype(F32)[0:1]
        here, before, lead = block_masks(docs, near[2 * rows :, 0 : 2 * rows].astype(F32)[0:1], None)
        for b in range(2):
            tri[b] = same_and_past(docs[:, b * rows : b * rows + rows], here[b])
            keep[b, 0:rows, :] = (before[1] == lead[b]).astype(BF16)
            keep[b, rows : 2 * rows, :] = (before[2] == lead[b]).astype(BF16)
            target[b] = (here[b] == lead[b]).astype(F32)
        keep[1, 2 * rows :, :] = (here[0] == lead[1]).astype(BF16)
        doc_ends[0] = before[2][rows - 8 :]
        doc_ends[1] = here[0][0:8]

    blank = jnp.zeros((rows, LANES), BF16)
    own_rim = packet[2 * rows :, :].astype(F32)
    near_rim = near[2 * rows :, :].astype(F32)
    rim_rows(rim, own_rim[8:], near_rim[0:8], doc_ends[0], doc_ends[1], short_filter, first_group, groups)
    tiles = out.shape[1] // LANES
    for tile in range(tiles):
        cols = slice(tile * LANES, tile * LANES + LANES)
        scratch = taps.at[tile % taps.shape[0]]
        masked = diag.at[tile % taps.shape[0]]
        build_middle(scratch, masked, tri, strips, first_group + tile * groups, groups, rows)
        added = rim[:, cols]
        lower, inner = own_products(masked, packet, added, cols, rows)
        source = near[0 : 2 * rows, cols]
        paired = jnp.concatenate(
            [
                jnp.concatenate([blank, source * keep[0, 0 : 2 * rows]], 0),
                jnp.concatenate([source, lower], 0) * keep[1],
            ],
            1,
        )
        outer = jnp.dot(scratch[...], paired, preferred_element_type=F32)
        for b in range(2):
            out[b * rows : b * rows + rows, cols] = (
                picked(inner, b, groups, rows) + target[b] * picked(outer, b, groups, rows)
            )


def build_rest(scratch, strips, first, groups, rows):
    lanes = lax.broadcasted_iota(jnp.int32, (SLAB, LANES), 1)
    for g in range(groups):
        for slab in range(rows // SLAB):
            at = g * rows + slab * SLAB
            begin = rows - SLAB * slab
            wide = strips[first + g, :, begin : begin + 3 * rows]
            scratch[at : at + SLAB, 0:rows] = jnp.where(lanes < 8, wide[:, 2 * rows :], wide[:, 0:rows])
            scratch[at : at + SLAB, rows:] = wide[:, rows : 2 * rows]


def ready_kernel(core, strips, after, taps, groups, first_group):
    for tile in range(taps.shape[0]):
        build_rest(taps.at[tile], strips, first_group + tile * groups, groups, taps.shape[1] // groups)


def rest_kernel(core, strips, packet, near, far, short_filter, gate_long, sums, *refs, groups, first_group, part, built):
    out_own, out_sib, taps, keep, target, total, doc_ends, rim = refs[-8:]
    short_filter = half_filters(core, short_filter)
    rows = far.shape[0] - SLAB
    step = pl.program_id(0)

    @pl.when(step == 0)
    def _():
        docs = packet[2 * rows :, 0 : 2 * rows].astype(F32)[0:1]
        far_docs = far[rows:, 0 : 2 * rows].astype(F32)[0:1]
        here, before, lead = block_masks(docs, near[2 * rows :, 0 : 2 * rows].astype(F32)[0:1], far_docs)
        end, summed = far_state(far_docs)
        for b in range(2):
            keep[b, 0:rows, :] = ((before[0] == lead[b]) & ~summed).astype(BF16)
            target[b] = (here[b] == lead[b]).astype(F32)
            target[2 + b] = ((here[b] == end) & summed).astype(F32)
            doc_ends[2 + b] = (before[1] == lead[b]).astype(F32)[0:8]
        doc_ends[0] = before[0][rows - 8 :]
        doc_ends[1] = before[1][0:8]

    near_rim = near[2 * rows :, :].astype(F32)
    far_rim = far[rows:, :].astype(F32)
    rim_rows(rim, near_rim[8:], far_rim[0:8], doc_ends[0], doc_ends[1], short_filter, first_group, groups)
    tiles = far.shape[1] // LANES
    for tile in range(tiles):
        cols = slice(tile * LANES, tile * LANES + LANES)
        if built:
            scratch = strips.at[tile]
        else:
            scratch = taps.at[tile % taps.shape[0]]
            build_rest(scratch, strips, first_group + tile * groups, groups, rows)
        added = rim[:, cols]
        spread = [
            jnp.concatenate([added * doc_ends[2 + b], jnp.zeros((rows - 8, LANES), F32)], 0).astype(BF16)
            for b in range(2)
        ]
        source = far[0:rows, cols]
        paired = jnp.concatenate(
            [
                jnp.concatenate([spread[0], source * keep[0]], 0),
                jnp.concatenate([source * keep[1], spread[1]], 0),
            ],
            1,
        )
        result = jnp.dot(scratch[...], paired, preferred_element_type=F32)
        total[0:rows, cols] = (
            sums[0:rows, cols] + target[0] * picked(result, 0, groups, rows) + target[2] * source.astype(F32)
        )
        total[rows:, cols] = sums[rows:, cols] + target[1] * picked(result, 1, groups, rows)
        total[rows : rows + 8, cols] += target[3, 0:8] * far_rim[8:, cols]
    share = far.shape[1]
    at = pl.multiple_of((PARTS * core[0] + part) * share, LANES)
    hand_out(core, total, gate_long[:, pl.ds(at, share)], out_own, out_sib)


def join_kernel(core, *refs):
    out = refs[-1]
    step = pl.program_id(0)
    for part in range(PARTS):

        @pl.when(step // (pl.num_programs(0) // PARTS) == part)
        def _():
            width = out.shape[1]
            at = pl.multiple_of((PARTS * (1 - core[0]) + part) * width, LANES)
            out[...] = (refs[PARTS][:, pl.ds(at, width)].astype(F32) * refs[part][...].astype(F32)).astype(BF16)


def body(gate_short, key_short, value_short, gate_long, doc_ids, se_filter, long_filter):
    rows, chans = gate_short.shape
    tap_count, filters = se_filter.shape
    reach = long_filter.shape[1]
    count = lax.axis_size("ctx")
    half = chans // 2
    share = half // PARTS
    group_width = chans // filters
    groups = LANES // group_width
    block, steps = share, 1
    width = reach + 2 * rows
    core = lax.rem(lax.axis_index("ctx"), 2).astype(jnp.int32).reshape(1)

    swap = [(i, i ^ 1) for i in range(count)]
    ahead = [(i, i + 2) for i in range(count - 2)]
    ahead_two = [(i, i + 4) for i in range(count - 4)]

    def send(value, links):
        return lax.ppermute(value, "ctx", links)

    def shape(*sizes):
        return pltpu.HBM(sizes, BF16)

    def stay(value):
        return pltpu.with_memory_space_constraint(value, pltpu.HBM)

    ahead_of = pl.Buffered(1)

    def whole(sizes):
        return pl.BlockSpec(sizes, lambda i, c: (0,) * len(sizes))

    def mine(height, part):
        return pl.BlockSpec(
            (height, block), lambda i, c: (0, (PARTS * c[0] + part) * steps + i), pipeline_mode=ahead_of
        )

    def local(height):
        return pl.BlockSpec((height, block), lambda i, c: (0, i))

    strip_spec = whole((filters // 2, SLAB, width))
    anywhere = pl.BlockSpec(memory_space=pl.ANY)
    short_spec = pl.BlockSpec((tap_count, filters // 2), lambda i, c: (0, c[0]))

    def call(kernel, name, grid, in_specs, out_specs, out_shape, scratch=(), aliases=None):
        return functools.partial(
            pl.pallas_call(
                kernel,
                grid_spec=pltpu.PrefetchScalarGridSpec(
                    num_scalar_prefetch=1, grid=grid, in_specs=in_specs, out_specs=out_specs, scratch_shapes=scratch
                ),
                out_shape=out_shape,
                input_output_aliases=aliases or {},
                compiler_params=pltpu.CompilerParams(vmem_limit_bytes=LIMIT),
                name=name,
            ),
            core,
        )

    gate_short, key_short, value_short = map(stay, (gate_short, key_short, value_short))
    docs = stay(doc_ids.reshape(1, rows))
    se_near, se_filter = se_filter, stay(se_filter)

    def begin(part):
        return send(
            call(
                pack_kernel,
                "pack",
                (steps,),
                [
                    pl.BlockSpec(
                        (rows, block),
                        lambda i, c: (0, (PARTS * (1 - c[0]) + part) * steps + i),
                        pipeline_mode=ahead_of,
                    )
                ]
                * 3
                + [whole((1, rows))],
                local(2 * rows + SLAB),
                shape(2 * rows + SLAB, share),
            )(key_short, value_short, gate_short, docs),
            swap,
        )

    def short(part, sibling, after):
        return call(
            functools.partial(short_kernel, groups=groups, first_group=part * (share // group_width)),
            "short",
            (steps,),
            [
                whole((1, rows)),
                mine(rows, part),
                mine(rows, part),
                mine(rows, part),
                local(2 * rows + SLAB),
                short_spec,
            ]
            + [anywhere] * len(after),
            [local(2 * rows + SLAB)] * 2,
            [shape(2 * rows + SLAB, share), jax.ShapeDtypeStruct((2 * rows + SLAB, share), BF16)],
            [
                pltpu.VMEM((8 + 2 * rows, block), F32),
                pltpu.VMEM((2 * rows, block), F32),
                pltpu.VMEM((tap_count, 2 * rows, LANES), F32),
                pltpu.VMEM((8 + 2 * rows, LANES), F32),
            ],
        )(docs, key_short, value_short, gate_short, sibling, se_filter, *after)

    def far_packet(part, strips, packet, after):
        return call(
            functools.partial(far_kernel, groups=groups, first_group=part * (share // group_width)),
            "far",
            (steps,),
            [strip_spec, local(2 * rows + SLAB)] + [anywhere] * len(after),
            local(rows + SLAB),
            shape(rows + SLAB, share),
            [
                pltpu.VMEM((block // LANES, groups * rows, 2 * rows), BF16),
                pltpu.VMEM((2 * rows, LANES), BF16),
            ],
        )(strips, packet, *after)

    def out_spec(part):
        return pl.BlockSpec((rows, block), lambda i, c: (0, (PARTS * c[0] + part) * steps + i))

    def middle(part, strips, packet, near, after):
        return call(
            functools.partial(middle_kernel, groups=groups, first_group=part * (share // group_width)),
            "middle",
            (steps,),
            [strip_spec, local(2 * rows + SLAB), local(2 * rows + SLAB), whole((tap_count, filters))]
            + [anywhere] * len(after),
            local(2 * rows),
            jax.ShapeDtypeStruct((2 * rows, share), F32),
            [
                pltpu.VMEM((2, groups * rows, 3 * rows), BF16),
                pltpu.VMEM((2, groups * rows, 2 * rows), BF16),
                pltpu.VMEM((2, rows, rows), BF16),
                pltpu.VMEM((2, 3 * rows, LANES), BF16),
                pltpu.VMEM((2, rows, LANES), F32),
                pltpu.VMEM((2, 8, LANES), F32),
                pltpu.VMEM((8, share), F32),
            ],
        )(strips, packet, near, se_near, *after)

    def ready(part, strips, after):
        size = (share // LANES, groups * rows, 2 * rows)
        return call(
            functools.partial(ready_kernel, groups=groups, first_group=part * (share // group_width)),
            "ready",
            (1,),
            [strip_spec, anywhere],
            whole(size),
            jax.ShapeDtypeStruct(size, BF16),
        )(strips, after)

    def rest(part, strips, packet, near, far, sums, begun, after):
        return call(
            functools.partial(rest_kernel, groups=groups, first_group=part * (share // group_width), part=part, built=part > 0),
            "rest",
            (steps,),
            [
                whole(strips.shape),
                local(2 * rows + SLAB),
                local(2 * rows + SLAB),
                local(rows + SLAB),
                whole((tap_count, filters)),
                whole((rows, chans)),
                local(2 * rows),
            ]
            + [anywhere] * len(begun + after),
            [out_spec(part), local(rows)],
            [shape(rows, chans), shape(rows, share)],
            [
                pltpu.VMEM((2, groups * rows if part == 0 else SLAB, 2 * rows), BF16),
                pltpu.VMEM((2, rows, LANES), BF16),
                pltpu.VMEM((4, rows, LANES), F32),
                pltpu.VMEM((2 * rows, block), F32),
                pltpu.VMEM((4, 8, LANES), F32),
                pltpu.VMEM((8, share), F32),
            ],
            aliases={8: 0} if begun else None,
        )(strips, packet, near, far, se_near, gate_long, sums, *begun, *after)

    def join(got, begun):
        there = pl.BlockSpec((rows, block), lambda i, c: (0, PARTS * steps * (1 - c[0]) + i))

        def got_spec(part):
            return pl.BlockSpec((rows, block), lambda i, c: (0, jnp.clip(i - part * steps, 0, steps - 1)))

        return call(
            join_kernel,
            "join",
            (PARTS * steps,),
            [got_spec(part) for part in range(PARTS)] + [whole((rows, chans)), anywhere],
            there,
            shape(rows, chans),
            aliases={2 + PARTS: 0},
        )(*got, gate_long, begun)

    siblings = [begin(part) for part in range(PARTS)]
    sendable, packets = zip(*[short(part, siblings[part], []) for part in range(PARTS)])
    nears = [send(packet, ahead) for packet in sendable]
    strips = call(
        strip_kernel,
        "strips",
        (1,),
        [pl.BlockSpec((filters // 2, reach), lambda i, c: (c[0], 0)), anywhere],
        strip_spec,
        jax.ShapeDtypeStruct((filters // 2, SLAB, width), BF16),
    )(long_filter, stay(sendable[-1]))
    fars = []
    for part in range(PARTS):
        beyond = far_packet(part, strips, packets[part], [])
        fars.append(send(beyond, ahead_two))
    sums_b = middle(1, strips, packets[1], nears[1], ())
    taps = ready(1, strips, sums_b)
    sums_a = middle(0, strips, packets[0], nears[0], (taps,))
    out, other_a = rest(0, strips, packets[0], nears[0], fars[0], sums_a, (), (sums_b,))
    got_a = send(other_a, swap)
    out, other_b = rest(1, taps, packets[1], nears[1], fars[1], sums_b, (out,), ())
    return join([got_a, send(other_b, swap)], out)


def solution(mesh):
    placed = (
        P(("groups", "ctx"), None),
        P(("groups", "ctx"), None),
        P(("groups", "ctx"), None),
        P(("groups", "ctx"), None),
        P(("groups", "ctx")),
        P(),
        P(),
    )
    return jax.shard_map(
        body, mesh=mesh, in_specs=placed, out_specs=P(("groups", "ctx"), None), check_vma=False
    )
```

```python
import functools

import jax
import jax.numpy as jnp
from jax import lax
from jax.experimental import pallas as pl
from jax.experimental.pallas import tpu as pltpu
from jax.sharding import PartitionSpec as P

F32 = jnp.float32
BF16 = jnp.bfloat16
SLAB = 16
LANES = 128
LIMIT = 32 * 1024 * 1024
PARTS = 2


def column(row):
    width = row.shape[1]
    return jnp.transpose(jnp.broadcast_to(row.astype(F32), (width, width)))


def pick(parts):
    lane_group = lax.broadcasted_iota(jnp.int32, parts[0].shape, 1) // (LANES // len(parts))
    out = parts[0]
    for index in range(1, len(parts)):
        out = jnp.where(lane_group == index, parts[index], out)
    return out


def widen(short_filter, first, groups):
    taps = short_filter.shape[0]
    lane = lax.broadcasted_iota(jnp.int32, (8, LANES), 1) // (LANES // groups)
    padded = jnp.concatenate([short_filter[...], jnp.zeros((8 - taps, LANES), F32)], 0)
    return jnp.take_along_axis(padded, lane + first, axis=1, mode="promise_in_bounds")


def rim_sum(tail, tail_docs, docs, taps, tap_count):
    line = lax.broadcasted_iota(jnp.int32, (8, LANES), 0)
    total = jnp.zeros((8, LANES), F32)
    for k in range(1, tap_count):
        same = (pltpu.roll(tail_docs, k, 0) == docs) & (line < k)
        total = total + jnp.where(same, pltpu.roll(tail, k, 0), 0.0) * taps[k : k + 1, :]
    return total


def rim_rows(out, gates, tail, tail_docs, docs, short_filter, first_group, groups):
    for tile in range(out.shape[1] // LANES):
        cols = slice(tile * LANES, tile * LANES + LANES)
        taps = widen(short_filter, first_group + tile * groups, groups)
        out[:, cols] = gates[:, cols] * rim_sum(tail[:, cols], tail_docs, docs, taps, short_filter.shape[0])


def build(taps, strips, first, groups, rows, width):
    for g in range(groups):
        for s in range(rows // SLAB):
            at = g * rows + s * SLAB
            begin = rows - SLAB * s
            taps[at : at + SLAB, 0:width] = strips[first + g, :, begin : begin + width]


def pack_kernel(core, key, value, gate, docs, out):
    rows, width = key.shape
    out[0:rows, :] = (key[...].astype(F32) * value[...].astype(F32)).astype(BF16)
    out[rows : 2 * rows, :] = gate[...]
    out[2 * rows :, 0:rows] = jnp.broadcast_to(docs[...].astype(F32), (SLAB, rows)).astype(BF16)
    out[2 * rows :, rows:] = jnp.zeros((SLAB, width - rows), BF16)


def strip_kernel(core, filters, after, out):
    count, reach = filters.shape
    lane = lax.broadcasted_iota(jnp.int32, (count, LANES), 1)
    turned = []
    for at in range(reach - LANES, -1, -LANES):
        piece = filters[:, at : at + LANES].astype(F32)
        turned.append(jnp.take_along_axis(piece, LANES - 1 - lane, axis=1, mode="promise_in_bounds"))
    blank = jnp.zeros((count, LANES), F32)
    lags = jnp.concatenate([blank] + turned + [blank], 1).astype(BF16)
    for g in range(count):
        row = jnp.broadcast_to(lags[g : g + 1, :], (SLAB, lags.shape[1]))
        out[g] = pltpu.roll(row, 1, 1, stride=1, stride_axis=0)


def short_kernel(core, docs, key, value, gate, sib, short_filter, *refs, groups, first_group):
    out, packet, kv_rows, gate_rows, agree, doc_rows = refs[-6:]
    step = pl.program_id(0)
    rows, width = key.shape
    tap_count = short_filter.shape[0]
    docs_own = docs[...].astype(F32)
    docs_sib = sib[2 * rows :, 0:rows].astype(F32)[0:1]
    mine = pl.multiple_of(core[0] * rows, rows)
    other = pl.multiple_of((1 - core[0]) * rows, rows)

    @pl.when(step == 0)
    def _():
        doc_rows[0:8, :] = jnp.full((8, LANES), -1.0, F32)
        doc_rows[pl.ds(8 + mine, rows), :] = column(docs_own)
        doc_rows[pl.ds(8 + other, rows), :] = column(docs_sib)
        here = doc_rows[8 : 8 + 2 * rows, :]
        for k in range(1, tap_count):
            agree[k] = (doc_rows[8 - k : 8 - k + 2 * rows, :] == here).astype(F32)
        kv_rows[0:8, :] = jnp.zeros((8, width), F32)

    kv_rows[pl.ds(8 + mine, rows), :] = (key[...].astype(F32) * value[...].astype(F32)).astype(BF16).astype(F32)
    kv_rows[pl.ds(8 + other, rows), :] = sib[0:rows, :].astype(F32)
    gate_rows[pl.ds(mine, rows), :] = gate[...].astype(F32)
    gate_rows[pl.ds(other, rows), :] = sib[rows : 2 * rows, :].astype(F32)
    for tile in range(width // LANES):
        cols = slice(tile * LANES, tile * LANES + LANES)
        taps = widen(short_filter, first_group + (step * (width // LANES) + tile) * groups, groups)
        total = kv_rows[8 : 8 + 2 * rows, cols] * taps[0:1]
        for k in range(1, tap_count):
            total = total + agree[k] * kv_rows[8 - k : 8 - k + 2 * rows, cols] * taps[k : k + 1]
        packet[0 : 2 * rows, cols] = (gate_rows[:, cols] * total).astype(BF16)
    first = jnp.where(core[0] == 0, docs_own, docs_sib)
    second = jnp.where(core[0] == 0, docs_sib, docs_own)
    line = lax.broadcasted_iota(jnp.int32, (8, width), 0)
    doc_line = jnp.concatenate([first, second, jnp.zeros((1, width - 2 * rows), F32)], 1)
    tail = jnp.where(line == 0, jnp.broadcast_to(doc_line, (8, width)), kv_rows[2 * rows : 2 * rows + 8, :])
    packet[2 * rows :, :] = jnp.concatenate([tail, gate_rows[0:8, :]], 0).astype(BF16)
    out[...] = packet[...]


def far_kernel(core, strips, packet, *refs, groups, first_group):
    out, taps, keep = refs[-3:]
    rows = packet.shape[0] // 2 - SLAB // 2
    docs = packet[2 * rows :, 0 : 2 * rows].astype(F32)[0:1]
    last = jnp.broadcast_to(docs[:, 2 * rows - 1 :], (rows, LANES))
    summed = jnp.broadcast_to(docs[:, rows + 7 : rows + 8], (rows, LANES)) == last
    tail = packet[2 * rows :, :].astype(F32)[0:8]

    @pl.when(pl.program_id(0) == 0)
    def _():
        keep[0:rows, :] = (column(docs[:, 0:rows]) == last).astype(BF16)
        keep[rows:, :] = (column(docs[:, rows:]) == last).astype(BF16)

    for tile in range(out.shape[1] // LANES):
        cols = slice(tile * LANES, tile * LANES + LANES)
        build(taps.at[tile], strips, first_group + tile * groups, groups, rows, 2 * rows)
        mixed = packet[0 : 2 * rows, cols]
        kept = mixed * keep[...]
        result = jnp.dot(taps[tile], kept, preferred_element_type=F32)
        total = pick([result[g * rows : g * rows + rows] for g in range(groups)])
        out[0:rows, cols] = jnp.where(summed, total, mixed[rows:].astype(F32)).astype(BF16)
        nearest = jnp.concatenate([taps[tile, g * rows : g * rows + SLAB, 0:rows] for g in range(groups)], 0)
        result = jnp.dot(nearest, kept[rows:], preferred_element_type=F32)
        more = pick([result[g * SLAB : g * SLAB + SLAB] for g in range(groups)])[0:8]
        out[rows:, cols] = jnp.concatenate([tail[:, cols], more], 0).astype(BF16)


def block_masks(docs, near_docs, far_docs):
    rows = docs.shape[1] // 2
    here = [column(docs[:, 0:rows]), column(docs[:, rows:])]
    before = [None if far_docs is None else column(far_docs[:, rows:])]
    before += [column(near_docs[:, 0:rows]), column(near_docs[:, rows:])]
    lead = [jnp.broadcast_to(docs[:, b * rows : b * rows + 1], (rows, LANES)) for b in range(2)]
    return here, before, lead


def same_and_past(docs, col):
    rows = docs.shape[1]
    position = lax.broadcasted_iota(jnp.int32, (rows, rows), 0)
    source = lax.broadcasted_iota(jnp.int32, (rows, rows), 1)
    same = col == jnp.broadcast_to(docs, (rows, rows))
    return jnp.where(same & (source <= position), 1.0, 0.0).astype(BF16)


def far_state(far_docs):
    rows = far_docs.shape[1] // 2
    end = jnp.broadcast_to(far_docs[:, 2 * rows - 1 :], (rows, LANES))
    return end, jnp.broadcast_to(far_docs[:, rows + 7 : rows + 8], (rows, LANES)) == end


def build_middle(scratch, masked, tri, strips, first, groups, rows):
    for g in range(groups):
        for slab in range(rows // SLAB):
            at = g * rows + slab * SLAB
            begin = 2 * rows - SLAB * slab
            wide = strips[first + g, :, begin : begin + 4 * rows]
            scratch[at : at + SLAB, :] = wide[:, 0 : 3 * rows]
            inside = wide[:, 3 * rows :]
            for b in range(2):
                side = slice(b * rows, b * rows + rows)
                masked[at : at + SLAB, side] = inside * tri[b, slab * SLAB : slab * SLAB + SLAB, :]


def own_products(masked, packet, added, cols, rows):
    lower = packet[0:rows, cols].astype(F32)
    lower = jnp.concatenate([lower[0:8] + added, lower[8:]], 0).astype(BF16)
    blank = jnp.zeros((rows, LANES), BF16)
    paired = jnp.concatenate(
        [jnp.concatenate([lower, blank], 0), jnp.concatenate([blank, packet[rows : 2 * rows, cols]], 0)], 1
    )
    return lower, jnp.dot(masked[...], paired, preferred_element_type=F32)


def picked(result, b, groups, rows):
    side = slice(b * LANES, b * LANES + LANES)
    return pick([result[g * rows : g * rows + rows, side] for g in range(groups)])


def half_filters(core, short_filter):
    width = short_filter.shape[1] // 2
    return short_filter[:, pl.ds(pl.multiple_of(core[0] * width, LANES), width)]


def hand_out(core, total, gate_own, out_own, out_sib):
    rows = gate_own.shape[0]
    mine = pl.multiple_of(core[0] * rows, rows)
    other = pl.multiple_of((1 - core[0]) * rows, rows)
    out_own[...] = (gate_own[...].astype(F32) * total[pl.ds(mine, rows), :]).astype(BF16)
    out_sib[...] = total[pl.ds(other, rows), :].astype(BF16)


def middle_kernel(core, strips, packet, near, short_filter, *refs, groups, first_group):
    out, taps, diag, tri, keep, target, doc_ends, rim = refs[-8:]
    short_filter = half_filters(core, short_filter)
    rows = out.shape[0] // 2
    step = pl.program_id(0)

    @pl.when(step == 0)
    def _():
        docs = packet[2 * rows :, 0 : 2 * rows].astype(F32)[0:1]
        here, before, lead = block_masks(docs, near[2 * rows :, 0 : 2 * rows].astype(F32)[0:1], None)
        for b in range(2):
            tri[b] = same_and_past(docs[:, b * rows : b * rows + rows], here[b])
            keep[b, 0:rows, :] = (before[1] == lead[b]).astype(BF16)
            keep[b, rows : 2 * rows, :] = (before[2] == lead[b]).astype(BF16)
            target[b] = (here[b] == lead[b]).astype(F32)
        keep[1, 2 * rows :, :] = (here[0] == lead[1]).astype(BF16)
        doc_ends[0] = before[2][rows - 8 :]
        doc_ends[1] = here[0][0:8]

    blank = jnp.zeros((rows, LANES), BF16)
    own_rim = packet[2 * rows :, :].astype(F32)
    near_rim = near[2 * rows :, :].astype(F32)
    rim_rows(rim, own_rim[8:], near_rim[0:8], doc_ends[0], doc_ends[1], short_filter, first_group, groups)
    tiles = out.shape[1] // LANES
    for tile in range(tiles):
        cols = slice(tile * LANES, tile * LANES + LANES)
        scratch = taps.at[tile % taps.shape[0]]
        masked = diag.at[tile % taps.shape[0]]
        build_middle(scratch, masked, tri, strips, first_group + tile * groups, groups, rows)
        added = rim[:, cols]
        lower, inner = own_products(masked, packet, added, cols, rows)
        source = near[0 : 2 * rows, cols]
        paired = jnp.concatenate(
            [
                jnp.concatenate([blank, source * keep[0, 0 : 2 * rows]], 0),
                jnp.concatenate([source, lower], 0) * keep[1],
            ],
            1,
        )
        outer = jnp.dot(scratch[...], paired, preferred_element_type=F32)
        for b in range(2):
            out[b * rows : b * rows + rows, cols] = (
                picked(inner, b, groups, rows) + target[b] * picked(outer, b, groups, rows)
            )


def build_rest(scratch, strips, first, groups, rows):
    lanes = lax.broadcasted_iota(jnp.int32, (SLAB, LANES), 1)
    for g in range(groups):
        for slab in range(rows // SLAB):
            at = g * rows + slab * SLAB
            begin = rows - SLAB * slab
            wide = strips[first + g, :, begin : begin + 3 * rows]
            scratch[at : at + SLAB, 0:rows] = jnp.where(lanes < 8, wide[:, 2 * rows :], wide[:, 0:rows])
            scratch[at : at + SLAB, rows:] = wide[:, rows : 2 * rows]


def ready_kernel(core, strips, after, taps, groups, first_group):
    for tile in range(taps.shape[0]):
        build_rest(taps.at[tile], strips, first_group + tile * groups, groups, taps.shape[1] // groups)


def rest_kernel(core, strips, packet, near, far, short_filter, gate_long, sums, *refs, groups, first_group, part, built):
    out_own, out_sib, taps, keep, target, total, doc_ends, rim = refs[-8:]
    short_filter = half_filters(core, short_filter)
    rows = far.shape[0] - SLAB
    step = pl.program_id(0)

    @pl.when(step == 0)
    def _():
        docs = packet[2 * rows :, 0 : 2 * rows].astype(F32)[0:1]
        far_docs = far[rows:, 0 : 2 * rows].astype(F32)[0:1]
        here, before, lead = block_masks(docs, near[2 * rows :, 0 : 2 * rows].astype(F32)[0:1], far_docs)
        end, summed = far_state(far_docs)
        for b in range(2):
            keep[b, 0:rows, :] = ((before[0] == lead[b]) & ~summed).astype(BF16)
            target[b] = (here[b] == lead[b]).astype(F32)
            target[2 + b] = ((here[b] == end) & summed).astype(F32)
            doc_ends[2 + b] = (before[1] == lead[b]).astype(F32)[0:8]
        doc_ends[0] = before[0][rows - 8 :]
        doc_ends[1] = before[1][0:8]

    near_rim = near[2 * rows :, :].astype(F32)
    far_rim = far[rows:, :].astype(F32)
    rim_rows(rim, near_rim[8:], far_rim[0:8], doc_ends[0], doc_ends[1], short_filter, first_group, groups)
    tiles = far.shape[1] // LANES
    for tile in range(tiles):
        cols = slice(tile * LANES, tile * LANES + LANES)
        if built:
            scratch = strips.at[tile]
        else:
            scratch = taps.at[tile % taps.shape[0]]
            build_rest(scratch, strips, first_group + tile * groups, groups, rows)
        added = rim[:, cols]
        spread = [
            jnp.concatenate([added * doc_ends[2 + b], jnp.zeros((rows - 8, LANES), F32)], 0).astype(BF16)
            for b in range(2)
        ]
        source = far[0:rows, cols]
        paired = jnp.concatenate(
            [
                jnp.concatenate([spread[0], source * keep[0]], 0),
                jnp.concatenate([source * keep[1], spread[1]], 0),
            ],
            1,
        )
        result = jnp.dot(scratch[...], paired, preferred_element_type=F32)
        total[0:rows, cols] = (
            sums[0:rows, cols] + target[0] * picked(result, 0, groups, rows) + target[2] * source.astype(F32)
        )
        total[rows:, cols] = sums[rows:, cols] + target[1] * picked(result, 1, groups, rows)
        total[rows : rows + 8, cols] += target[3, 0:8] * far_rim[8:, cols]
    share = far.shape[1]
    at = pl.multiple_of((PARTS * core[0] + part) * share, LANES)
    hand_out(core, total, gate_long[:, pl.ds(at, share)], out_own, out_sib)


def join_kernel(core, *refs):
    out = refs[-1]
    step = pl.program_id(0)
    for part in range(PARTS):

        @pl.when(step // (pl.num_programs(0) // PARTS) == part)
        def _():
            width = out.shape[1]
            at = pl.multiple_of((PARTS * (1 - core[0]) + part) * width, LANES)
            out[...] = (refs[PARTS][:, pl.ds(at, width)].astype(F32) * refs[part][...].astype(F32)).astype(BF16)


def body(gate_short, key_short, value_short, gate_long, doc_ids, se_filter, long_filter):
    rows, chans = gate_short.shape
    tap_count, filters = se_filter.shape
    reach = long_filter.shape[1]
    count = lax.axis_size("ctx")
    half = chans // 2
    share = half // PARTS
    group_width = chans // filters
    groups = LANES // group_width
    block, steps = share, 1
    width = reach + 2 * rows
    core = lax.rem(lax.axis_index("ctx"), 2).astype(jnp.int32).reshape(1)

    swap = [(i, i ^ 1) for i in range(count)]
    ahead = [(i, i + 2) for i in range(count - 2)]
    ahead_two = [(i, i + 4) for i in range(count - 4)]

    def send(value, links):
        return lax.ppermute(value, "ctx", links)

    def shape(*sizes):
        return pltpu.HBM(sizes, BF16)

    def stay(value):
        return pltpu.with_memory_space_constraint(value, pltpu.HBM)

    ahead_of = pl.Buffered(1)

    def whole(sizes):
        return pl.BlockSpec(sizes, lambda i, c: (0,) * len(sizes))

    def mine(height, part):
        return pl.BlockSpec(
            (height, block), lambda i, c: (0, (PARTS * c[0] + part) * steps + i), pipeline_mode=ahead_of
        )

    def local(height):
        return pl.BlockSpec((height, block), lambda i, c: (0, i))

    strip_spec = whole((filters // 2, SLAB, width))
    anywhere = pl.BlockSpec(memory_space=pl.ANY)
    short_spec = pl.BlockSpec((tap_count, filters // 2), lambda i, c: (0, c[0]))

    def call(kernel, name, grid, in_specs, out_specs, out_shape, scratch=(), aliases=None):
        return functools.partial(
            pl.pallas_call(
                kernel,
                grid_spec=pltpu.PrefetchScalarGridSpec(
                    num_scalar_prefetch=1, grid=grid, in_specs=in_specs, out_specs=out_specs, scratch_shapes=scratch
                ),
                out_shape=out_shape,
                input_output_aliases=aliases or {},
                compiler_params=pltpu.CompilerParams(vmem_limit_bytes=LIMIT),
                name=name,
            ),
            core,
        )

    gate_short, key_short, value_short = map(stay, (gate_short, key_short, value_short))
    docs = stay(doc_ids.reshape(1, rows))
    se_near, se_filter = se_filter, stay(se_filter)

    def begin(part):
        return send(
            call(
                pack_kernel,
                "pack",
                (steps,),
                [
                    pl.BlockSpec(
                        (rows, block),
                        lambda i, c: (0, (PARTS * (1 - c[0]) + part) * steps + i),
                        pipeline_mode=ahead_of,
                    )
                ]
                * 3
                + [whole((1, rows))],
                local(2 * rows + SLAB),
                shape(2 * rows + SLAB, share),
            )(key_short, value_short, gate_short, docs),
            swap,
        )

    def short(part, sibling, after):
        piece = pl.BlockSpec((2 * rows + SLAB, share // 2), lambda i, c: (0, i))
        ours = pl.BlockSpec((rows, share // 2), lambda i, c: (0, (PARTS * c[0] + part) * 2 + i))
        return call(
            functools.partial(short_kernel, groups=groups, first_group=part * (share // group_width)),
            "short",
            (2,),
            [
                whole((1, rows)),
                ours,
                ours,
                ours,
                piece,
                short_spec,
            ]
            + [anywhere] * len(after),
            [piece] * 2,
            [shape(2 * rows + SLAB, share), jax.ShapeDtypeStruct((2 * rows + SLAB, share), BF16)],
            [
                pltpu.VMEM((8 + 2 * rows, share // 2), F32),
                pltpu.VMEM((2 * rows, share // 2), F32),
                pltpu.VMEM((tap_count, 2 * rows, LANES), F32),
                pltpu.VMEM((8 + 2 * rows, LANES), F32),
            ],
        )(docs, key_short, value_short, gate_short, sibling, se_filter, *after)

    def far_packet(part, strips, packet, after):
        return call(
            functools.partial(far_kernel, groups=groups, first_group=part * (share // group_width)),
            "far",
            (steps,),
            [strip_spec, local(2 * rows + SLAB)] + [anywhere] * len(after),
            local(rows + SLAB),
            shape(rows + SLAB, share),
            [
                pltpu.VMEM((block // LANES, groups * rows, 2 * rows), BF16),
                pltpu.VMEM((2 * rows, LANES), BF16),
            ],
        )(strips, packet, *after)

    def out_spec(part):
        return pl.BlockSpec((rows, block), lambda i, c: (0, (PARTS * c[0] + part) * steps + i))

    def middle(part, strips, packet, near, after):
        return call(
            functools.partial(middle_kernel, groups=groups, first_group=part * (share // group_width)),
            "middle",
            (steps,),
            [strip_spec, local(2 * rows + SLAB), local(2 * rows + SLAB), whole((tap_count, filters))]
            + [anywhere] * len(after),
            local(2 * rows),
            jax.ShapeDtypeStruct((2 * rows, share), F32),
            [
                pltpu.VMEM((2, groups * rows, 3 * rows), BF16),
                pltpu.VMEM((2, groups * rows, 2 * rows), BF16),
                pltpu.VMEM((2, rows, rows), BF16),
                pltpu.VMEM((2, 3 * rows, LANES), BF16),
                pltpu.VMEM((2, rows, LANES), F32),
                pltpu.VMEM((2, 8, LANES), F32),
                pltpu.VMEM((8, share), F32),
            ],
        )(strips, packet, near, se_near, *after)

    def ready(part, strips, after):
        size = (share // LANES, groups * rows, 2 * rows)
        return call(
            functools.partial(ready_kernel, groups=groups, first_group=part * (share // group_width)),
            "ready",
            (1,),
            [strip_spec, anywhere],
            whole(size),
            jax.ShapeDtypeStruct(size, BF16),
        )(strips, after)

    def rest(part, strips, packet, near, far, sums, begun, after):
        return call(
            functools.partial(rest_kernel, groups=groups, first_group=part * (share // group_width), part=part, built=part > 0),
            "rest",
            (steps,),
            [
                whole(strips.shape),
                local(2 * rows + SLAB),
                local(2 * rows + SLAB),
                local(rows + SLAB),
                whole((tap_count, filters)),
                whole((rows, chans)),
                local(2 * rows),
            ]
            + [anywhere] * len(begun + after),
            [out_spec(part), local(rows)],
            [shape(rows, chans), shape(rows, share)],
            [
                pltpu.VMEM((2, groups * rows if part == 0 else SLAB, 2 * rows), BF16),
                pltpu.VMEM((2, rows, LANES), BF16),
                pltpu.VMEM((4, rows, LANES), F32),
                pltpu.VMEM((2 * rows, block), F32),
                pltpu.VMEM((4, 8, LANES), F32),
                pltpu.VMEM((8, share), F32),
            ],
            aliases={8: 0} if begun else None,
        )(strips, packet, near, far, se_near, gate_long, sums, *begun, *after)

    def join(got, begun):
        there = pl.BlockSpec((rows, block), lambda i, c: (0, PARTS * steps * (1 - c[0]) + i))

        def got_spec(part):
            return pl.BlockSpec((rows, block), lambda i, c: (0, jnp.clip(i - part * steps, 0, steps - 1)))

        return call(
            join_kernel,
            "join",
            (PARTS * steps,),
            [got_spec(part) for part in range(PARTS)] + [whole((rows, chans)), anywhere],
            there,
            shape(rows, chans),
            aliases={2 + PARTS: 0},
        )(*got, gate_long, begun)

    siblings = [begin(part) for part in range(PARTS)]
    sendable, packets = zip(*[short(part, siblings[part], []) for part in range(PARTS)])
    nears = [send(packet, ahead) for packet in sendable]
    strips = call(
        strip_kernel,
        "strips",
        (1,),
        [pl.BlockSpec((filters // 2, reach), lambda i, c: (c[0], 0)), anywhere],
        strip_spec,
        jax.ShapeDtypeStruct((filters // 2, SLAB, width), BF16),
    )(long_filter, stay(sendable[-1]))
    fars = []
    for part in range(PARTS):
        beyond = far_packet(part, strips, packets[part], [])
        fars.append(send(beyond, ahead_two))
    sums_b = middle(1, strips, packets[1], nears[1], ())
    taps = ready(1, strips, sums_b)
    sums_a = middle(0, strips, packets[0], nears[0], (taps,))
    out, other_a = rest(0, strips, packets[0], nears[0], fars[0], sums_a, (), (sums_b,))
    got_a = send(other_a, swap)
    out, other_b = rest(1, taps, packets[1], nears[1], fars[1], sums_b, (out,), ())
    return join([got_a, send(other_b, swap)], out)


def solution(mesh):
    placed = (
        P(("groups", "ctx"), None),
        P(("groups", "ctx"), None),
        P(("groups", "ctx"), None),
        P(("groups", "ctx"), None),
        P(("groups", "ctx")),
        P(),
        P(),
    )
    return jax.shard_map(
        body, mesh=mesh, in_specs=placed, out_specs=P(("groups", "ctx"), None), check_vma=False
    )
```
